128 devices in a mesh: tm: 8 (over z_hi, x), gx: 16 (over z_lo, y, core).
Axes of the slice: x: 4, y: 4, z: 4 (z_hi: 2, z_lo: 2; z = z_hi * 2 + z_lo), core: 2. Of those that a mesh axis runs over, the one named last changes fastest.
Arguments:
- state: float32 [16, 64, 256, 128], P('tm', 'gx'), may hold values from -3 to 3
- start_field: float32 [64, 256, 128], P('gx'), may hold values from -3 to 3
- diffusivity: float32 [64, 256, 128], P('gx'), may hold values from 0.3 to 3
- time_weights: float32 [16], P('tm'), may hold values from 0.4 to 1
- shift_real: float32 [16], replicated, may hold values from 0.5 to 2, as said below
- shift_imag: float32 [16], replicated, may hold values from -1 to 1, as said below
Outputs:
- new_state: float32 [16, 64, 256, 128], P('tm', 'gx')
The draws below stay inside these ranges and needn't reach their ends.
Inputs may be any that keep to these rules, and one draw needn't show every extreme that they name: `shift_real`: shift_real_k = shift_real_(16 - k) for k = 1 .. 15. `shift_imag`: shift_imag_0 = shift_imag_(8) = 0 and shift_imag_k = - shift_imag_(16 - k), so the eigenvalues come in conjugate pairs.
All inputs are finite; a program needn't handle non-finite values.
Results may differ from the reference program's by a relative error of at most 0.0003.
Values sent between devices are 32-bit elements; how exact they have to be, the bound alone decides.
A program may use at most 64 MiB of HBM per device.

```python
import math
import jax
import jax.numpy as jnp
from jax import lax

STEPS = 16
CY = 256
CZ = 128
SWEEPS = 12
NX = 64


def folded_modes():
    position = jnp.arange(STEPS)
    return (position, jnp.minimum(position, STEPS - position))


def draw_shift_real(key, part):
    half_count = STEPS // 2 + 1
    base_values = jnp.exp(jax.random.uniform(jax.random.fold_in(key, 11), (half_count,), jnp.float32, math.log(0.5), math.log(2.0)))
    position, folded = folded_modes()
    return base_values[folded].astype(jnp.float32)


def draw_shift_imag(key, part):
    half_count = STEPS // 2 + 1
    base_values = jax.random.uniform(jax.random.fold_in(key, 23), (half_count,), jnp.float32, -1.0, 1.0)
    position, folded = folded_modes()
    flipped = jnp.where(position > STEPS // 2, -1.0, 1.0).astype(jnp.float32)
    inside = (folded > 0) & (folded < STEPS // 2)
    return jnp.where(inside, base_values[folded] * flipped, 0.0).astype(jnp.float32)


def shard_levels(key, shape, pieces, smallest, high):
    def one(dim, blocks):
        draws = jax.random.uniform(jax.random.fold_in(jax.random.fold_in(key, 6), dim), (blocks,), jnp.float32, smallest / len(pieces), high / len(pieces))
        return jnp.repeat(jnp.exp(draws), shape[dim] // blocks).reshape((-1,) + (1,) * (len(shape) - dim - 1))

    loudness = one(*pieces[0])
    for cut in pieces[1:]:
        loudness = loudness * one(*cut)
    return loudness


def noise(key, shape, deviation, limit, pieces=(), dtype=jnp.bfloat16):
    entries = jax.random.normal(key, shape, jnp.float32) * deviation
    if len(pieces) > 0:
        entries = shard_levels(key, shape, pieces, -0.22, 0.18) * entries
    return jnp.clip(entries, min=-limit, max=limit).astype(dtype)


def setup_inputs(seed: int = 0) -> dict:
    streams_of = jax.random.split(jax.random.key(seed), 7)
    return {
        "state": noise(streams_of[0], (STEPS, NX, CY, CZ), 0.5, 3.0, ((0, 8), (1, 16)), jnp.float32),
        "start_field": noise(streams_of[1], (NX, CY, CZ), 0.5, 3.0, ((0, 16),), jnp.float32),
        "diffusivity": jnp.clip(jnp.exp(math.log(3.0) - 2.3025851 * jax.random.uniform(streams_of[2], (NX, CY, CZ), jnp.float32) ** shard_levels(streams_of[2], (NX, CY, CZ), ((0, 16),), -0.2, 0.2)), 0.3, 3.0),
        "time_weights": jnp.clip(jnp.exp(math.log(1.0) - 0.9162907 * jax.random.uniform(streams_of[3], (STEPS,), jnp.float32) ** shard_levels(streams_of[3], (STEPS,), ((0, 8),), -0.2, 0.2)), 0.4, 1.0),
        "shift_real": draw_shift_real(jax.random.fold_in(streams_of[6], 71), 0),
        "shift_imag": draw_shift_imag(jax.random.fold_in(streams_of[6], 71), 0),
    }


cheb_centre = 1.0
cheb_half = 0.7


def along(core, axis, lower):
    length = core.shape[axis]
    zeros = jnp.zeros_like(lax.slice_in_dim(core, 0, 1, axis=axis))
    if lower:
        return jnp.concatenate([zeros, lax.slice_in_dim(core, 0, length - 1, axis=axis)], axis)
    return jnp.concatenate([lax.slice_in_dim(core, 1, length, axis=axis), zeros], axis)


def six_near(padded):
    core = padded[..., 1:-1, :, :]
    rank = core.ndim
    return core, (padded[..., :-2, :, :], padded[..., 2:, :, :], along(core, rank - 2, True), along(core, rank - 2, False), along(core, rank - 1, True), along(core, rank - 1, False))


def operate(padded, faces, diag_sum):
    core, near = six_near(padded)
    total = faces[0] * near[0]
    for which in range(1, 6):
        total = total + faces[which] * near[which]
    return diag_sum * core - total


def pad_first(field):
    return jnp.pad(field, ((1, 1), (0, 0), (0, 0)))


def reference(state, start_field, diffusivity, time_weights, shift_real, shift_imag):
    kappa, near = six_near(pad_first(diffusivity))
    faces = [0.5 * (kappa + other) for other in near]
    diag_sum = faces[0]
    for which in range(1, 6):
        diag_sum = diag_sum + faces[which]
    prior = jnp.concatenate([start_field[None], state[:-1]], 0)

    def react(pair):
        now, before = pair
        applied = operate(pad_first(now), faces, diag_sum)
        return before - now - (applied + now * now * now - now)

    residual = lax.map(react, (state, prior))
    spectrum = jnp.fft.fft(time_weights[:, None, None, None] * residual, axis=0)

    def solve(inputs):
        source_real, source_imag, mode_real, mode_imag = inputs
        denom_real = mode_real + diag_sum
        magnitude = denom_real * denom_real + mode_imag * mode_imag
        inverse_real = denom_real / magnitude
        inverse_imag = -mode_imag / magnitude
        answer_real = source_real * inverse_real - source_imag * inverse_imag
        answer_imag = source_real * inverse_imag + source_imag * inverse_real
        for turn in range(SWEEPS):
            omega = 1.0 / (cheb_centre + cheb_half * math.cos(math.pi * (2 * turn + 1) / (2 * SWEEPS)))
            applied_real = operate(pad_first(answer_real), faces, diag_sum)
            applied_imag = operate(pad_first(answer_imag), faces, diag_sum)
            misfit_real = source_real - (mode_real * answer_real - mode_imag * answer_imag + applied_real)
            misfit_imag = source_imag - (mode_real * answer_imag + mode_imag * answer_real + applied_imag)
            answer_real = answer_real + omega * (misfit_real * inverse_real - misfit_imag * inverse_imag)
            answer_imag = answer_imag + omega * (misfit_real * inverse_imag + misfit_imag * inverse_real)
        return answer_real, answer_imag

    answer_real, answer_imag = lax.map(solve, (jnp.real(spectrum), jnp.imag(spectrum), shift_real, shift_imag))
    back = jnp.fft.ifft(answer_real + 1j * answer_imag, axis=0)
    return state + jnp.real(back) / time_weights[:, None, None, None]
```

```python
import functools
import math

import jax
import jax.numpy as jnp
from jax import lax
from jax.experimental import pallas as pl
from jax.experimental.pallas import tpu as pltpu
from jax.sharding import PartitionSpec as P

SWEEPS = 12
MESH = pl.DeviceIdType.MESH
F32 = jnp.float32
OMEGAS = [
    1.0 / (1.0 + 0.7 * math.cos(math.pi * (2 * turn + 1) / (2 * SWEEPS))) for turn in range(SWEEPS)
]

TMS = 8
PL = 4
ROWS = 32
EP = PL + 4
ER = ROWS + 4
F = 16
R = 2
NPH = 16 // R
STEPS2 = SWEEPS // 2
TILE_ORDER = (0, 3, 1, 2)
PEERS = ((0, 1), (0, 3), (1, 0), (1, 1), (1, 3), (0, 2), (1, 2))


def real_dft(values):
    n = len(values)
    if n == 2:
        return [(values[0] + values[1], None), (values[0] - values[1], None)]
    even = real_dft(values[0::2])
    odd = real_dft(values[1::2])
    half = n // 2
    out = [None] * (half + 1)
    for k in range(half // 2 + 1):
        er, ei = even[k]
        orr, oi = odd[k]
        if k == 0:
            out[0] = (er + orr, None)
            out[half] = (er - orr, None)
        elif 2 * k == half:
            out[k] = (er, -orr)
        else:
            c, s = math.cos(2 * math.pi * k / n), -math.sin(2 * math.pi * k / n)
            if oi is None:
                tr, ti = orr * c, orr * s
            else:
                tr, ti = orr * c - oi * s, orr * s + oi * c
            out[k] = (er + tr, ti if ei is None else ei + ti)
            out[half - k] = (er - tr, ti if ei is None else ti - ei)
    return out


def real_sum(modes, n):
    if n == 2:
        return [modes[0][0] + modes[1][0], modes[0][0] - modes[1][0]]
    half = n // 2
    even, odd = [], []
    for k in range(half // 2 + 1):
        ar, ai = modes[k]
        br, bi = modes[half - k]
        if k == 0:
            even.append((ar + br, None))
            odd.append((ar - br, None))
        elif 2 * k == half:
            even.append((ar + ar, None))
            odd.append((-(ai + ai), None))
        else:
            c, s = math.cos(2 * math.pi * k / n), math.sin(2 * math.pi * k / n)
            even.append((ar + br, ai - bi))
            dr, di = ar - br, ai + bi
            odd.append((dr * c - di * s, dr * s + di * c))
    e = real_sum(even, half)
    o = real_sum(odd, half)
    out = [None] * n
    out[0::2] = e
    out[1::2] = o
    return out


def snake(p):
    return jnp.where(p < 4, p, 11 - p)


def pick(table, index):
    value = jnp.float32(table[0])
    for i in range(1, len(table)):
        value = jnp.where(index == i, jnp.float32(table[i]), value)
    return value


def kernel(
    ngx,
    state,
    start,
    kappa,
    weights,
    shift_real,
    shift_imag,
    out,
    w,
    wb,
    sb,
    stage,
    first,
    kst,
    tws,
    shifts,
    fx,
    fy,
    fzl,
    fzu,
    dg,
    ia,
    ib,
    ic,
    loc,
    a_s,
    a_r,
    t_s,
    t_r,
    k_s,
    k_r,
    h_s,
    h_r,
    hy_s,
    hy_r,
    x_s,
    x_r,
    y_s,
    y_r,
    c_s,
    c_r,
    o_s,
    o_r,
    o_l,
):
    tm = lax.axis_index("tm")
    gx = lax.axis_index("gx")
    p = snake(tm)
    zh = tm // 4
    xx = lax.rem(tm, 4)
    peers = [lax.rem(zh + dz, 2) * 4 + lax.rem(xx + dx, 4) for dz, dx in PEERS]
    has_lo, has_hi = gx > 0, gx < ngx - 1
    has_dn, has_up = p > 0, p < TMS - 1
    gxs = (gx - 1, gx + 1)
    tms = (snake(p - 1), snake(p + 1))
    x_to = (has_lo, has_hi)
    x_from = (has_hi, has_lo)
    y_to = (has_dn, has_up)
    y_from = (has_up, has_dn)
    row0 = pl.multiple_of(p * ROWS, ROWS)

    barrier = pltpu.get_barrier_semaphore()
    for peer in peers:
        pl.semaphore_signal(barrier, inc=1, device_id=(peer, gx), device_id_type=MESH)
    for d in range(2):

        @pl.when(x_to[d])
        def _():
            pl.semaphore_signal(barrier, inc=1, device_id=(tm, gxs[d]), device_id_type=MESH)

        for e in range(2):

            @pl.when(x_to[d] & y_to[e])
            def _():
                pl.semaphore_signal(
                    barrier, inc=1, device_id=(tms[e], gxs[d]), device_id_type=MESH
                )

    nx = has_lo.astype(jnp.int32) + has_hi.astype(jnp.int32)
    ny = has_dn.astype(jnp.int32) + has_up.astype(jnp.int32)

    own = [
        pltpu.make_async_copy(
            state.at[:, :, pl.ds(row0, ROWS)], stage.at[pl.ds(2 * tm, 2)], loc.at[0]
        ),
        pltpu.make_async_copy(start.at[:, pl.ds(row0, ROWS)], first, loc.at[1]),
    ]
    for copy in own:
        copy.start()
    pieces = (
        (None, row0, 8, ROWS),
        (has_dn, pl.multiple_of(jnp.maximum(row0 - 8, 0), 8), 0, 8),
        (has_up, pl.multiple_of(jnp.minimum(row0 + ROWS, (TMS - 1) * ROWS), 8), 8 + ROWS, 8),
    )

    def guarded(condition, body):
        if condition is None:
            body()
        else:
            pl.when(condition)(body)

    def kappa_own(i):
        _, r, at, n = pieces[i]
        return pltpu.make_async_copy(
            kappa.at[:, pl.ds(r, n)], kst.at[pl.ds(2, PL), pl.ds(at, n)], loc.at[2 + i]
        )

    def kappa_out(d, i):
        _, r, at, n = pieces[i]
        return pltpu.make_async_remote_copy(
            kappa.at[pl.ds(2 * d, 2), pl.ds(r, n)],
            kst.at[pl.ds(6 if d == 0 else 0, 2), pl.ds(at, n)],
            k_s.at[d, i],
            k_r.at[d, i],
            device_id=(tm, gxs[d]),
            device_id_type=MESH,
        )

    for i in range(3):
        guarded(pieces[i][0], lambda i=i: kappa_own(i).start())

    for i in range(2):
        tws[2 * tm + i] = jnp.full((8, 128), weights[i], F32)

    pl.semaphore_wait(barrier, 7 + nx + nx * ny)

    def tile_out(j, tile):
        rows = pl.multiple_of(snake(peers[j]) * ROWS + 8 * tile, 8)
        return pltpu.make_async_remote_copy(
            state.at[:, :, pl.ds(rows, 8)],
            stage.at[pl.ds(2 * tm, 2), :, pl.ds(8 * tile, 8)],
            a_s.at[j, tile],
            a_r.at[j, tile],
            device_id=(peers[j], gx),
            device_id_type=MESH,
        )

    def weight_out(j):
        return pltpu.make_async_remote_copy(
            tws.at[pl.ds(2 * tm, 2)],
            tws.at[pl.ds(2 * tm, 2)],
            t_s.at[j],
            t_r.at[j],
            device_id=(peers[j], gx),
            device_id_type=MESH,
        )

    for d in range(2):
        for i in range(3):
            condition = x_to[d] if pieces[i][0] is None else x_to[d] & pieces[i][0]
            guarded(condition, lambda d=d, i=i: kappa_out(d, i).start())
    for j in range(7):
        weight_out(j).start()
    for tile in TILE_ORDER:
        for j in range(7):
            tile_out(j, tile).start()

    def clear_planes(ref, base, at):
        def body(r, _):
            for i in range(2):
                ref[base + at + i, pl.ds(pl.multiple_of(r * 64, 64), 64)] = jnp.zeros((64, 128), F32)
            return 0

        lax.fori_loop(0, ER * F // 64, body, 0)

    def clear_rows(ref, base, at):
        def body(i, _):
            ref[base + i, pl.ds(at * F, 2 * F)] = jnp.zeros((2 * F, 128), F32)
            return 0

        lax.fori_loop(0, EP, body, 0)

    def clear(condition, planes, at):
        @pl.when(condition)
        def _():
            for i in range(3):
                (clear_planes if planes else clear_rows)(w, i * EP, at)
            (clear_planes if planes else clear_rows)(sb, 0, at)

    clear(gx == 0, True, 0)
    clear(gx == ngx - 1, True, EP - 2)
    clear(p == 0, False, 0)
    clear(p == TMS - 1, False, ER - 2)
    for condition, at in ((gx == 0, 0), (gx == ngx - 1, EP - 2)):

        @pl.when(condition)
        def _():
            kst[pl.ds(at, 2)] = jnp.zeros((2, ROWS + 16, 128), F32)

    for condition, at in ((p == 0, 0), (p == TMS - 1, 8 + ROWS)):

        @pl.when(condition)
        def _():
            kst[:, pl.ds(at, 8)] = jnp.zeros((EP, 8, 128), F32)

    lane = lax.broadcasted_iota(jnp.int32, (8, 128), 1)
    sub = lax.broadcasted_iota(jnp.int32, (8, 128), 0)
    s_a = jnp.full((8, 128), shift_real[0], F32)
    s_c = jnp.full((8, 128), shift_real[8], F32)
    s_i = jnp.zeros((8, 128), F32)
    for m in range(1, 8):
        s_a = jnp.where(sub == m, shift_real[m], s_a)
        s_c = jnp.where(sub == m, shift_real[m], s_c)
        s_i = jnp.where(sub == m, shift_imag[m], s_i)
    shifts[0] = s_a
    shifts[1] = s_c
    shifts[2] = s_i

    for i in range(3):
        guarded(pieces[i][0], lambda i=i: kappa_own(i).wait())
    for d in range(2):
        for i in range(3):
            cond_from = x_from[d] if pieces[i][0] is None else x_from[d] & pieces[i][0]
            cond_to = x_to[d] if pieces[i][0] is None else x_to[d] & pieces[i][0]
            guarded(cond_from, lambda d=d, i=i: kappa_out(d, i).wait_recv())
            guarded(cond_to, lambda d=d, i=i: kappa_out(d, i).wait_send())

    def coefficients(yi, _):
        at = pl.multiple_of(yi * 8, 8)

        def cell(px, dy):
            return jnp.broadcast_to(kst[px, pl.ds(yi + 6 + dy, 1), :], (8, 128))

        s_a, s_c, s_i = shifts[0], shifts[1], shifts[2]
        outside_y = ((p == 0) & (yi < 2)) | ((p == TMS - 1) & (yi > ER - 3))
        below, here = cell(0, 0), cell(1, 0)
        low = 0.5 * (here + below)
        for px in range(1, EP - 1):
            above = cell(px + 1, 0)
            high = 0.5 * (here + above)
            yl = 0.5 * (here + cell(px, -1))
            yu = 0.5 * (here + cell(px, 1))
            k_low = jnp.where(lane == 0, 0.0, pltpu.roll(here, 1, 1))
            k_high = jnp.where(lane == 127, 0.0, pltpu.roll(here, 127, 1))
            zl = 0.5 * (here + k_low)
            zu = 0.5 * (here + k_high)
            diag = low + high + yl + yu + zl + zu
            fx[px, pl.ds(at, 8)] = low
            if px == EP - 2:
                fx[px + 1, pl.ds(at, 8)] = high
            fy[px, pl.ds(at, 8)] = yl
            fy[px, pl.ds(pl.multiple_of(at + 8, 8), 8)] = yu
            fzl[px, pl.ds(at, 8)] = jnp.where(lane == 0, 0.0, zl)
            fzu[px, pl.ds(at, 8)] = jnp.where(lane == 127, 0.0, zu)
            dg[px, pl.ds(at, 8)] = diag
            outside = outside_y
            if px == 1:
                outside = outside | (gx == 0)
            if px == EP - 2:
                outside = outside | (gx == ngx - 1)
            inside = jnp.where(outside, 0.0, 1.0).astype(F32)
            d_a = s_a + diag
            ratio = inside / (d_a * d_a + s_i * s_i)
            ia[px, pl.ds(at, 8)] = d_a * ratio
            ib[px, pl.ds(at, 8)] = -s_i * ratio
            d_c = s_c + diag
            ic[px, pl.ds(at, 8)] = d_c * (inside / (d_c * d_c + s_i * s_i))
            here, low = above, high
        return 0

    lax.fori_loop(1, ER - 1, coefficients, 0)

    def forward(tile):
        rows = pl.multiple_of(tile * 8, 8)

        def plane(x, _):
            base = (8 * tile + 2) * F

            def put(ref, at, modes):
                for m in range(9):
                    re, im = modes[m]
                    if m == 8:
                        ref[at, pl.ds(base + 8, 8, stride=F), :] = re
                        continue
                    ref[at, pl.ds(base + m, 8, stride=F), :] = re
                    if m > 0:
                        ref[at, pl.ds(base + 8 + m, 8, stride=F), :] = im

            now = [stage[t, x, pl.ds(rows, 8), :] for t in range(16)]
            put(sb, x + 2, real_dft([tws[t] * now[t] for t in range(16)]))
            before = [first[x, pl.ds(rows, 8), :]] + now[:15]
            put(
                w,
                x + 2,
                real_dft([tws[t] * (before[t] - now[t] * now[t] * now[t]) for t in range(16)]),
            )
            return 0

        lax.fori_loop(0, PL, plane, 0)

    def h_copy(d, tile):
        rows = pl.ds(pl.multiple_of((8 * tile + 2) * F, 8), 8 * F)
        return pltpu.make_async_remote_copy(
            sb.at[2 if d == 0 else EP - 3, rows],
            sb.at[EP - 2 if d == 0 else 1, rows],
            h_s.at[d, tile],
            h_r.at[d, tile],
            device_id=(tm, gxs[d]),
            device_id_type=MESH,
        )

    def hy_copy(d):
        return pltpu.make_async_remote_copy(
            sb.at[pl.ds(2, PL), pl.ds((2 if d == 0 else ER - 3) * F, F)],
            sb.at[pl.ds(2, PL), pl.ds((ER - 2 if d == 0 else 1) * F, F)],
            hy_s.at[d],
            hy_r.at[d],
            device_id=(tms[d], gx),
            device_id_type=MESH,
        )

    def x_copy(buf, par, d, e, i):
        r = R * i if e == 0 else ROWS - R - R * i
        rows = pl.ds(pl.multiple_of((r + 2) * F, 8), R * F)
        return pltpu.make_async_remote_copy(
            w.at[pl.ds(buf + (2 if d == 0 else EP - 4), 2), rows],
            w.at[pl.ds(buf + (EP - 2 if d == 0 else 0), 2), rows],
            x_s.at[d, e, i],
            x_r.at[par, d, e, i],
            device_id=(tm, gxs[d]),
            device_id_type=MESH,
        )

    def y_copy(buf, par, d):
        return pltpu.make_async_remote_copy(
            w.at[pl.ds(buf + 2, PL), pl.ds((2 if d == 0 else ER - 4) * F, 2 * F)],
            w.at[pl.ds(buf + 2, PL), pl.ds((ER - 2 if d == 0 else 0) * F, 2 * F)],
            y_s.at[d],
            y_r.at[par, d],
            device_id=(tms[d], gx),
            device_id_type=MESH,
        )

    def c_copy(buf, par, d, e):
        return pltpu.make_async_remote_copy(
            w.at[buf + (2 if d == 0 else EP - 3), pl.ds((2 if e == 0 else ER - 3) * F, F)],
            w.at[buf + (EP - 2 if d == 0 else 1), pl.ds((ER - 2 if e == 0 else 1) * F, F)],
            c_s.at[d, e],
            c_r.at[par, d, e],
            device_id=(tms[e], gxs[d]),
            device_id_type=MESH,
        )

    def x_start(buf, par, i):
        for e in range(2):
            for d in range(2):
                pl.when(x_to[d])(lambda d=d, e=e: x_copy(buf, par, d, e, i).start())

    def x_wait_send(buf, par, i):
        for e in range(2):
            for d in range(2):
                pl.when(x_to[d])(lambda d=d, e=e: x_copy(buf, par, d, e, i).wait_send())

    def x_wait_recv(buf, par, i):
        for e in range(2):
            for d in range(2):
                pl.when(x_from[d])(lambda d=d, e=e: x_copy(buf, par, d, e, i).wait_recv())

    def edges_start(buf, par):
        for d in range(2):
            pl.when(y_to[d])(lambda d=d: y_copy(buf, par, d).start())
        for d in range(2):
            for e in range(2):
                pl.when(x_to[d] & y_to[e])(lambda d=d, e=e: c_copy(buf, par, d, e).start())

    def edges_wait_send(buf, par):
        for d in range(2):
            pl.when(y_to[d])(lambda d=d: y_copy(buf, par, d).wait_send())
        for d in range(2):
            for e in range(2):
                pl.when(x_to[d] & y_to[e])(lambda d=d, e=e: c_copy(buf, par, d, e).wait_send())

    def edges_wait_recv(buf, par):
        for d in range(2):
            pl.when(y_from[d])(lambda d=d: y_copy(buf, par, d).wait_recv())
        for d in range(2):
            for e in range(2):
                pl.when(x_from[d] & y_from[e])(
                    lambda d=d, e=e: c_copy(buf, par, d, e).wait_recv()
                )

    def row_parts(ref, base, yi, low, high):
        at = pl.multiple_of(yi * 8, 8)
        rows = [pl.multiple_of(yi * F + 8 * t, 8) for t in range(2)]

        def get(px, t, dy):
            return ref[base + px, pl.ds(pl.multiple_of(rows[t] + dy * F, 8), 8), :]

        below = [get(low - 1, t, 0) for t in range(2)]
        here = [get(low, t, 0) for t in range(2)]
        face_low = fx[low, pl.ds(at, 8)]
        for px in range(low, high):
            face_high = fx[px + 1, pl.ds(at, 8)]
            y_low = fy[px, pl.ds(at, 8)]
            y_high = fy[px, pl.ds(pl.multiple_of(at + 8, 8), 8)]
            z_low = fzl[px, pl.ds(at, 8)]
            z_high = fzu[px, pl.ds(at, 8)]
            sums = []
            above = []
            for t in range(2):
                up = get(px + 1, t, 0)
                above.append(up)
                total = face_low * below[t] + face_high * up
                total = total + (y_low * get(px, t, -1) + y_high * get(px, t, 1))
                total = total + (
                    z_low * pltpu.roll(here[t], 1, 1) + z_high * pltpu.roll(here[t], 127, 1)
                )
                sums.append(total)
            yield px, at, rows, here, sums
            below, here, face_low = here, above, face_high

    def divided(px, at, value):
        a, b, c = ia[px, pl.ds(at, 8)], ib[px, pl.ds(at, 8)], ic[px, pl.ds(at, 8)]
        return [a * value[0] - b * value[1], c * value[1] + b * value[0]]

    def starts(yi):
        results = []
        for px, at, rows, here, sums in row_parts(sb, 0, yi, 2, EP - 2):
            diag = dg[px, pl.ds(at, 8)]
            right = [
                w[px, pl.ds(rows[t], 8), :] - (diag * here[t] - sums[t]) for t in range(2)
            ]
            results.append((px, rows, divided(px, at, right)))
        for px, rows, value in results:
            for t in range(2):
                w[px, pl.ds(rows[t], 8), :] = value[t]

    def sweep(ref, base, target, target_base, yi, low, high, omega):
        results = []
        for px, at, rows, here, sums in row_parts(ref, base, yi, low, high):
            step = divided(px, at, sums)
            new = [
                (1.0 - omega) * here[t] + omega * (w[px, pl.ds(rows[t], 8), :] + step[t])
                for t in range(2)
            ]
            results.append((px, rows, new))
        for px, rows, value in results:
            for t in range(2):
                target[target_base + px, pl.ds(rows[t], 8), :] = value[t]

    def over(begin, count, body):
        def each(r, _):
            body(begin + r + 2)
            return 0

        lax.fori_loop(0, count, each, 0)

    def start_phase(i):
        over(R * i, R, starts)
        over(ROWS - R - R * i, R, starts)
        x_start(0, 0, i)

    for copy in own:
        copy.wait()
    for j in range(7):
        weight_out(j).wait_recv()
    for tiles in (TILE_ORDER[:2], TILE_ORDER[2:]):
        for tile in tiles:
            for j in range(7):
                tile_out(j, tile).wait_recv()
            forward(tile)
            for d in range(2):
                pl.when(x_to[d])(lambda d=d, tile=tile: h_copy(d, tile).start())
            if tile == 0:
                pl.when(y_to[0])(lambda: hy_copy(0).start())
            if tile == 3:
                pl.when(y_to[1])(lambda: hy_copy(1).start())
    for tiles in (TILE_ORDER[:2], TILE_ORDER[2:]):
        for tile in tiles:
            for d in range(2):
                pl.when(x_from[d])(lambda d=d, tile=tile: h_copy(d, tile).wait_recv())
            if tile == 0:
                pl.when(y_from[1])(lambda: hy_copy(1).wait_recv())
            if tile == 3:
                pl.when(y_from[0])(lambda: hy_copy(0).wait_recv())
        if tiles[0] == 0:
            start_phase(0)
            edges_start(0, 0)
            lax.fori_loop(1, NPH // 2, lambda i, _: (start_phase(i), 0)[1], 0)
        else:
            lax.fori_loop(NPH // 2, NPH, lambda i, _: (start_phase(i), 0)[1], 0)
    for tile in range(4):
        for d in range(2):
            pl.when(x_to[d])(lambda d=d, tile=tile: h_copy(d, tile).wait_send())
    for d in range(2):
        pl.when(y_to[d])(lambda d=d: hy_copy(d).wait_send())

    def home(tile, j):
        return pltpu.make_async_remote_copy(
            stage.at[pl.ds(2 * peers[j], 2), :, pl.ds(pl.multiple_of(8 * tile, 8), 8)],
            out.at[:, :, pl.ds(pl.multiple_of(row0 + 8 * tile, 8), 8)],
            o_s.at[j, tile],
            o_r.at[j, tile],
            device_id=(peers[j], gx),
            device_id_type=MESH,
        )

    def home_recv(tile, j):
        return pltpu.make_async_remote_copy(
            stage.at[pl.ds(2 * tm, 2), :, pl.ds(pl.multiple_of(8 * tile, 8), 8)],
            out.at[:, :, pl.ds(pl.multiple_of(snake(peers[j]) * ROWS + 8 * tile, 8), 8)],
            o_s.at[j, tile],
            o_r.at[j, tile],
            device_id=(peers[j], gx),
            device_id_type=MESH,
        )

    def home_own(tile):
        return pltpu.make_async_copy(
            stage.at[pl.ds(2 * tm, 2), :, pl.ds(pl.multiple_of(8 * tile, 8), 8)],
            out.at[:, :, pl.ds(pl.multiple_of(row0 + 8 * tile, 8), 8)],
            o_l.at[tile],
        )

    def backward(buf, tile):
        rows = pl.multiple_of(tile * 8, 8)

        def plane(x, _):
            base = (8 * tile + 2) * F
            field = [w[buf + x + 2, pl.ds(base + f, 8, stride=F), :] for f in range(F)]
            modes = [(field[0], None)]
            modes += [(field[m], field[8 + m]) for m in range(1, 8)]
            modes += [(field[8], None)]
            back = real_sum(modes, 16)
            for t in range(16):
                stage[t, x, pl.ds(rows, 8), :] = stage[t, x, pl.ds(rows, 8), :] + back[t] / (
                    16.0 * tws[t]
                )
            return 0

        lax.fori_loop(0, PL, plane, 0)
        for j in range(7):
            home(tile, j).start()
        home_own(tile).start()

    def two_sweeps(k, _):
        par = lax.rem(k, 2)
        source = jnp.where(k == 0, 0, (1 + par) * EP)
        result = (2 - par) * EP
        om_a = pick(OMEGAS[0::2], k)
        om_b = pick(OMEGAS[1::2], k)

        def first_sweep(begin, count):
            over(begin, count, lambda yi: sweep(w, source, wb, 0, yi, 1, EP - 1, om_a))

        def second_sweep(begin, count):
            over(begin, count, lambda yi: sweep(wb, 0, w, result, yi, 2, EP - 2, om_b))

        def pass_on(i):
            x_wait_send(result, par, i)

            @pl.when(k < STEPS2 - 1)
            def _():
                x_start(result, 1 - par, i)

        def finish(i):
            @pl.when(k == STEPS2 - 1)
            def _():
                backward(result, i)
                backward(result, 3 - i)

        edges_wait_recv(source, par)
        x_wait_recv(source, par, 0)
        x_wait_recv(source, par, 1)
        first_sweep(-1, R + 2)
        first_sweep(ROWS - 1 - R, R + 2)
        second_sweep(0, R)
        second_sweep(ROWS - R, R)
        pass_on(0)
        edges_wait_send(result, par)

        @pl.when(k < STEPS2 - 1)
        def _():
            edges_start(result, 1 - par)

        def phase(i, _):
            x_wait_recv(source, par, i + 1)
            first_sweep(R * i + 1, R)
            first_sweep(ROWS - 1 - R - R * i, R)
            second_sweep(R * i, R)
            second_sweep(ROWS - R - R * i, R)
            pass_on(i)

            @pl.when(i == NPH // 2 - 1)
            def _():
                finish(0)

            return 0

        lax.fori_loop(1, NPH - 1, phase, 0)
        first_sweep(17 - R, 2 * R - 2)
        second_sweep(16 - R, 2 * R)
        pass_on(NPH - 1)
        finish(1)
        return 0

    lax.fori_loop(0, STEPS2, two_sweeps, 0)

    for j in range(7):
        weight_out(j).wait_send()
        for tile in range(4):
            tile_out(j, tile).wait_send()
    for tile in TILE_ORDER:
        home_own(tile).wait()
        for j in range(7):
            home(tile, j).wait_send()
            home_recv(tile, j).wait_recv()


def shards(ngx, state, start_field, diffusivity, time_weights, shift_real, shift_imag):
    dma = pltpu.SemaphoreType.DMA
    any_space = pl.BlockSpec(memory_space=pl.ANY)
    smem = pl.BlockSpec(memory_space=pltpu.SMEM)
    coefficient = pltpu.VMEM((EP, ER * 8, 128), F32)
    return pl.pallas_call(
        functools.partial(kernel, ngx),
        out_shape=jax.ShapeDtypeStruct(state.shape, F32),
        in_specs=[any_space, any_space, any_space, smem, smem, smem],
        out_specs=any_space,
        scratch_shapes=[
            pltpu.VMEM((3 * EP, ER * F, 128), F32),
            pltpu.VMEM((EP, ER * F, 128), F32),
            pltpu.VMEM((EP, ER * F, 128), F32),
            pltpu.VMEM((16, PL, ROWS, 128), F32),
            pltpu.VMEM((PL, ROWS, 128), F32),
            pltpu.VMEM((EP, ROWS + 16, 128), F32),
            pltpu.VMEM((16, 8, 128), F32),
            pltpu.VMEM((3, 8, 128), F32),
        ]
        + [coefficient] * 8
        + [
            dma((5,)),
            dma((7, 4)),
            dma((7, 4)),
            dma((7,)),
            dma((7,)),
            dma((2, 3)),
            dma((2, 3)),
            dma((2, 4)),
            dma((2, 4)),
            dma((2,)),
            dma((2,)),
            dma((2, 2, NPH)),
            dma((2, 2, 2, NPH)),
            dma((2,)),
            dma((2, 2)),
            dma((2, 2)),
            dma((2, 2, 2)),
            dma((7, 4)),
            dma((7, 4)),
            dma((4,)),
        ],
        compiler_params=pltpu.CompilerParams(
            collective_id=0, has_side_effects=True, vmem_limit_bytes=44 * 2**20
        ),
        cost_estimate=pl.CostEstimate(
            flops=200_000_000, bytes_accessed=4 * 2**20, transcendentals=0
        ),
    )(state, start_field, diffusivity, time_weights, shift_real, shift_imag)


def solution(mesh):
    in_specs = (
        P("tm", "gx", None, None),
        P("gx", None, None),
        P("gx", None, None),
        P("tm"),
        P(),
        P(),
    )
    return jax.shard_map(
        functools.partial(shards, mesh.shape["gx"]),
        mesh=mesh,
        in_specs=in_specs,
        out_specs=P("tm", "gx", None, None),
        check_vma=False,
    )
```

```python
import functools
import math

import jax
import jax.numpy as jnp
from jax import lax
from jax.experimental import pallas as pl
from jax.experimental.pallas import tpu as pltpu
from jax.sharding import PartitionSpec as P

SWEEPS = 12
MESH = pl.DeviceIdType.MESH
F32 = jnp.float32
OMEGAS = [
    1.0 / (1.0 + 0.7 * math.cos(math.pi * (2 * turn + 1) / (2 * SWEEPS))) for turn in range(SWEEPS)
]

TMS = 8
PL = 4
ROWS = 32
H = 3
EP = PL + 2 * H
ER = ROWS + 2 * H
F = 16
R = 4
NPH = 16 // R
STEPS = SWEEPS // H
TILE_ORDER = (0, 3, 1, 2)
PEERS = ((0, 1), (0, 3), (1, 0), (1, 1), (1, 3), (0, 2), (1, 2))


def real_dft(values):
    n = len(values)
    if n == 2:
        return [(values[0] + values[1], None), (values[0] - values[1], None)]
    even = real_dft(values[0::2])
    odd = real_dft(values[1::2])
    half = n // 2
    out = [None] * (half + 1)
    for k in range(half // 2 + 1):
        er, ei = even[k]
        orr, oi = odd[k]
        if k == 0:
            out[0] = (er + orr, None)
            out[half] = (er - orr, None)
        elif 2 * k == half:
            out[k] = (er, -orr)
        else:
            c, s = math.cos(2 * math.pi * k / n), -math.sin(2 * math.pi * k / n)
            if oi is None:
                tr, ti = orr * c, orr * s
            else:
                tr, ti = orr * c - oi * s, orr * s + oi * c
            out[k] = (er + tr, ti if ei is None else ei + ti)
            out[half - k] = (er - tr, ti if ei is None else ti - ei)
    return out


def real_sum(modes, n):
    if n == 2:
        return [modes[0][0] + modes[1][0], modes[0][0] - modes[1][0]]
    half = n // 2
    even, odd = [], []
    for k in range(half // 2 + 1):
        ar, ai = modes[k]
        br, bi = modes[half - k]
        if k == 0:
            even.append((ar + br, None))
            odd.append((ar - br, None))
        elif 2 * k == half:
            even.append((ar + ar, None))
            odd.append((-(ai + ai), None))
        else:
            c, s = math.cos(2 * math.pi * k / n), math.sin(2 * math.pi * k / n)
            even.append((ar + br, ai - bi))
            dr, di = ar - br, ai + bi
            odd.append((dr * c - di * s, dr * s + di * c))
    e = real_sum(even, half)
    o = real_sum(odd, half)
    out = [None] * n
    out[0::2] = e
    out[1::2] = o
    return out


def snake(p):
    return jnp.where(p < 4, p, 11 - p)


def pick(table, index):
    value = jnp.float32(table[0])
    for i in range(1, len(table)):
        value = jnp.where(index == i, jnp.float32(table[i]), value)
    return value


def kernel(
    ngx,
    state,
    start,
    kappa,
    weights_in,
    shift_real_in,
    shift_imag_in,
    out,
    weights,
    shift_real,
    shift_imag,
    w,
    w0,
    wb,
    sb,
    stage,
    first,
    kst,
    tws,
    shifts,
    fx,
    fy,
    fzl,
    fzu,
    dg,
    ia,
    ib,
    ic,
    loc,
    a_s,
    a_r,
    t_s,
    t_r,
    k_s,
    k_r,
    h_s,
    h_r,
    hy_s,
    hy_r,
    x_s,
    x_r,
    y_s,
    y_r,
    c_s,
    c_r,
    o_s,
    o_r,
    o_l,
    passing,
    passing_row,
    p_s,
    p_r,
):
    tm = lax.axis_index("tm")
    gx = lax.axis_index("gx")
    p = snake(tm)
    zh = tm // 4
    xx = lax.rem(tm, 4)
    peers = [lax.rem(zh + dz, 2) * 4 + lax.rem(xx + dx, 4) for dz, dx in PEERS]
    has_lo, has_hi = gx > 0, gx < ngx - 1
    has_dn, has_up = p > 0, p < TMS - 1
    gxs = (gx - 1, gx + 1)
    tms = (snake(p - 1), snake(p + 1))
    x_to = (has_lo, has_hi)
    x_from = (has_hi, has_lo)
    y_to = (has_dn, has_up)
    y_from = (has_up, has_dn)
    row0 = pl.multiple_of(p * ROWS, ROWS)

    turning = (tm == 3) | (tm == 7)
    side = jnp.where(gx < ngx // 2, gx + ngx // 2, gx - ngx // 2)
    side_pair = side + 1 - 2 * lax.rem(side, 2)
    at_end = (gx < 2) | (gx >= ngx - 2)
    relayed = tuple(at_end & (tm == turn) for turn in (7, 3))
    relaying = tuple((gx >= ngx // 2 - 2) & (gx < ngx // 2 + 2) & (tm == turn) for turn in (3, 7))
    even = lax.rem(gx, 2) == 0
    c_to = [
        [
            x_to[d] & y_to[e] & jnp.logical_not(relayed[e] & (even if d == 1 else ~even))
            for e in range(2)
        ]
        for d in range(2)
    ]

    barrier = pltpu.get_barrier_semaphore()
    for peer in peers:
        pl.semaphore_signal(barrier, inc=1, device_id=(peer, gx), device_id_type=MESH)
    for d in range(2):

        @pl.when(x_to[d])
        def _():
            pl.semaphore_signal(barrier, inc=1, device_id=(tm, gxs[d]), device_id_type=MESH)

        for e in range(2):

            @pl.when(x_to[d] & y_to[e])
            def _():
                pl.semaphore_signal(
                    barrier, inc=1, device_id=(tms[e], gxs[d]), device_id_type=MESH
                )

    in_relay = turning & (at_end | ((gx >= ngx // 2 - 2) & (gx < ngx // 2 + 2)))

    @pl.when(in_relay)
    def _():
        for there in ((10 - tm, side), (tm, side), (tm, side_pair)):
            pl.semaphore_signal(barrier, inc=1, device_id=there, device_id_type=MESH)

    nx = has_lo.astype(jnp.int32) + has_hi.astype(jnp.int32)
    ny = has_dn.astype(jnp.int32) + has_up.astype(jnp.int32)

    own = [
        pltpu.make_async_copy(
            state.at[:, :, pl.ds(row0, ROWS)], stage.at[pl.ds(2 * tm, 2)], loc.at[0]
        ),
        pltpu.make_async_copy(start.at[:, pl.ds(row0, ROWS)], first, loc.at[1]),
    ]
    scalars = [
        pltpu.make_async_copy(source, target, loc.at[5 + i])
        for i, (source, target) in enumerate(
            ((weights_in, weights), (shift_real_in, shift_real), (shift_imag_in, shift_imag))
        )
    ]
    for copy in scalars + own:
        copy.start()
    pieces = (
        (None, row0, 8, ROWS),
        (has_dn, pl.multiple_of(jnp.maximum(row0 - 8, 0), 8), 0, 8),
        (has_up, pl.multiple_of(jnp.minimum(row0 + ROWS, (TMS - 1) * ROWS), 8), 8 + ROWS, 8),
    )

    def guarded(condition, body):
        if condition is None:
            body()
        else:
            pl.when(condition)(body)

    def kappa_own(i):
        _, r, at, n = pieces[i]
        return pltpu.make_async_copy(
            kappa.at[:, pl.ds(r, n)], kst.at[pl.ds(H, PL), pl.ds(at, n)], loc.at[2 + i]
        )

    def kappa_out(d, i):
        _, r, at, n = pieces[i]
        return pltpu.make_async_remote_copy(
            kappa.at[pl.ds(0 if d == 0 else PL - H, H), pl.ds(r, n)],
            kst.at[pl.ds(EP - H if d == 0 else 0, H), pl.ds(at, n)],
            k_s.at[d, i],
            k_r.at[d, i],
            device_id=(tm, gxs[d]),
            device_id_type=MESH,
        )

    for i in range(3):
        guarded(pieces[i][0], lambda i=i: kappa_own(i).start())

    pl.semaphore_wait(barrier, 7 + nx + nx * ny + 3 * in_relay.astype(jnp.int32))

    def tile_out(j, tile):
        rows = pl.multiple_of(snake(peers[j]) * ROWS + 8 * tile, 8)
        return pltpu.make_async_remote_copy(
            state.at[:, :, pl.ds(rows, 8)],
            stage.at[pl.ds(2 * tm, 2), :, pl.ds(8 * tile, 8)],
            a_s.at[j, tile],
            a_r.at[j, tile],
            device_id=(peers[j], gx),
            device_id_type=MESH,
        )

    def weight_out(j):
        return pltpu.make_async_remote_copy(
            tws.at[pl.ds(2 * tm, 2)],
            tws.at[pl.ds(2 * tm, 2)],
            t_s.at[j],
            t_r.at[j],
            device_id=(peers[j], gx),
            device_id_type=MESH,
        )

    for d in range(2):
        for i in range(3):
            condition = x_to[d] if pieces[i][0] is None else x_to[d] & pieces[i][0]
            guarded(condition, lambda d=d, i=i: kappa_out(d, i).start())
    for tile in TILE_ORDER:
        for j in range(7):
            tile_out(j, tile).start()
        if tile == 0:
            for copy in scalars:
                copy.wait()
            for i in range(2):
                tws[2 * tm + i] = jnp.full((8, 128), weights[i], F32)
            for j in range(7):
                weight_out(j).start()

    def clear_planes(ref, base, at):
        def body(r, _):
            for i in range(H):
                ref[base + at + i, pl.ds(pl.multiple_of(r * 32, 32), 32)] = jnp.zeros((32, 128), F32)
            return 0

        lax.fori_loop(0, ER * F // 32, body, 0)

    def clear_rows(ref, base, at):
        def body(i, _):
            ref[base + i, pl.ds(at * F, H * F)] = jnp.zeros((H * F, 128), F32)
            return 0

        lax.fori_loop(0, EP, body, 0)

    def clear(condition, planes, at):
        @pl.when(condition)
        def _():
            for i in range(2):
                (clear_planes if planes else clear_rows)(w, i * EP, at)
            (clear_planes if planes else clear_rows)(w0, 0, at)
            (clear_planes if planes else clear_rows)(sb, 0, at)

    clear(gx == 0, True, 0)
    clear(gx == ngx - 1, True, EP - H)
    clear(p == 0, False, 0)
    clear(p == TMS - 1, False, ER - H)
    for condition, at in ((gx == 0, 0), (gx == ngx - 1, EP - H)):

        @pl.when(condition)
        def _():
            kst[pl.ds(at, H)] = jnp.zeros((H, ROWS + 16, 128), F32)

    for condition, at in ((p == 0, 0), (p == TMS - 1, 8 + ROWS)):

        @pl.when(condition)
        def _():
            kst[:, pl.ds(at, 8)] = jnp.zeros((EP, 8, 128), F32)

    lane = lax.broadcasted_iota(jnp.int32, (8, 128), 1)
    sub = lax.broadcasted_iota(jnp.int32, (8, 128), 0)
    s_a = jnp.full((8, 128), shift_real[0], F32)
    s_c = jnp.full((8, 128), shift_real[8], F32)
    s_i = jnp.zeros((8, 128), F32)
    for m in range(1, 8):
        s_a = jnp.where(sub == m, shift_real[m], s_a)
        s_c = jnp.where(sub == m, shift_real[m], s_c)
        s_i = jnp.where(sub == m, shift_imag[m], s_i)
    shifts[0] = s_a
    shifts[1] = s_c
    shifts[2] = s_i

    for i in range(3):
        guarded(pieces[i][0], lambda i=i: kappa_own(i).wait())
    for d in range(2):
        for i in range(3):
            cond_from = x_from[d] if pieces[i][0] is None else x_from[d] & pieces[i][0]
            cond_to = x_to[d] if pieces[i][0] is None else x_to[d] & pieces[i][0]
            guarded(cond_from, lambda d=d, i=i: kappa_out(d, i).wait_recv())
            guarded(cond_to, lambda d=d, i=i: kappa_out(d, i).wait_send())

    def coefficients(yi, _):
        at = pl.multiple_of(yi * 8, 8)

        def cell(px, dy):
            return jnp.broadcast_to(kst[px, pl.ds(yi + 8 - H + dy, 1), :], (8, 128))

        s_a, s_c, s_i = shifts[0], shifts[1], shifts[2]
        outside_y = ((p == 0) & (yi < H)) | ((p == TMS - 1) & (yi > ER - 1 - H))
        below, here = cell(0, 0), cell(1, 0)
        low = 0.5 * (here + below)
        for px in range(1, EP - 1):
            above = cell(px + 1, 0)
            high = 0.5 * (here + above)
            yl = 0.5 * (here + cell(px, -1))
            yu = 0.5 * (here + cell(px, 1))
            k_low = jnp.where(lane == 0, 0.0, pltpu.roll(here, 1, 1))
            k_high = jnp.where(lane == 127, 0.0, pltpu.roll(here, 127, 1))
            zl = 0.5 * (here + k_low)
            zu = 0.5 * (here + k_high)
            diag = low + high + yl + yu + zl + zu
            fx[px, pl.ds(at, 8)] = low
            if px == EP - 2:
                fx[px + 1, pl.ds(at, 8)] = high
            fy[px, pl.ds(at, 8)] = yl
            fy[px, pl.ds(pl.multiple_of(at + 8, 8), 8)] = yu
            fzl[px, pl.ds(at, 8)] = jnp.where(lane == 0, 0.0, zl)
            fzu[px, pl.ds(at, 8)] = jnp.where(lane == 127, 0.0, zu)
            dg[px, pl.ds(at, 8)] = diag
            outside = outside_y
            if px < H:
                outside = outside | (gx == 0)
            if px > EP - 1 - H:
                outside = outside | (gx == ngx - 1)
            inside = jnp.where(outside, 0.0, 1.0).astype(F32)
            d_a = s_a + diag
            ratio = inside / (d_a * d_a + s_i * s_i)
            ia[px, pl.ds(at, 8)] = d_a * ratio
            ib[px, pl.ds(at, 8)] = -s_i * ratio
            d_c = s_c + diag
            ic[px, pl.ds(at, 8)] = d_c * (inside / (d_c * d_c + s_i * s_i))
            here, low = above, high
        return 0

    lax.fori_loop(1, ER - 1, coefficients, 0)

    def forward(tile):
        rows = pl.multiple_of(tile * 8, 8)

        def plane(x, _):
            base = (8 * tile + H) * F

            def put(ref, at, modes):
                for m in range(9):
                    re, im = modes[m]
                    if m == 8:
                        ref[at, pl.ds(base + 8, 8, stride=F), :] = re
                        continue
                    ref[at, pl.ds(base + m, 8, stride=F), :] = re
                    if m > 0:
                        ref[at, pl.ds(base + 8 + m, 8, stride=F), :] = im

            now = [stage[t, x, pl.ds(rows, 8), :] for t in range(16)]
            put(sb, x + H, real_dft([tws[t] * now[t] for t in range(16)]))
            before = [first[x, pl.ds(rows, 8), :]] + now[:15]
            put(
                w0,
                x + H,
                real_dft([tws[t] * (before[t] - now[t] * now[t] * now[t]) for t in range(16)]),
            )
            return 0

        lax.fori_loop(0, PL, plane, 0)

    def h_copy(d, tile):
        rows = pl.ds(pl.multiple_of((8 * tile + H) * F, 8), 8 * F)
        return pltpu.make_async_remote_copy(
            sb.at[H if d == 0 else EP - 1 - H, rows],
            sb.at[EP - H if d == 0 else H - 1, rows],
            h_s.at[d, tile],
            h_r.at[d, tile],
            device_id=(tm, gxs[d]),
            device_id_type=MESH,
        )

    def hy_copy(d):
        return pltpu.make_async_remote_copy(
            sb.at[pl.ds(H, PL), pl.ds((H if d == 0 else ER - 1 - H) * F, F)],
            sb.at[pl.ds(H, PL), pl.ds((ER - H if d == 0 else H - 1) * F, F)],
            hy_s.at[d],
            hy_r.at[d],
            device_id=(tms[d], gx),
            device_id_type=MESH,
        )

    def hy_relay(d):
        return pltpu.make_async_remote_copy(
            sb.at[pl.ds(H, PL), pl.ds((H if d == 0 else ER - 1 - H) * F, F)],
            passing_row,
            hy_s.at[d],
            p_r.at[STEPS],
            device_id=(10 - tm, side),
            device_id_type=MESH,
        )

    def hy_forward(d):
        return pltpu.make_async_remote_copy(
            passing_row,
            sb.at[pl.ds(H, PL), pl.ds((ER - H if d == 0 else H - 1) * F, F)],
            p_s.at[2],
            hy_r.at[d],
            device_id=(tm, side),
            device_id_type=MESH,
        )

    def hy_start(d):
        pl.when(y_to[d] & ~relayed[d])(lambda: hy_copy(d).start())
        pl.when(relayed[d])(lambda: hy_relay(d).start())

    def x_copy(ref, buf, par, d, e, i):
        r = R * i if e == 0 else ROWS - R - R * i
        rows = pl.ds(pl.multiple_of((r + H) * F, 8), R * F)
        return pltpu.make_async_remote_copy(
            ref.at[pl.ds(buf + (H if d == 0 else PL), H), rows],
            ref.at[pl.ds(buf + (EP - H if d == 0 else 0), H), rows],
            x_s.at[d, e, i],
            x_r.at[par, d, e, i],
            device_id=(tm, gxs[d]),
            device_id_type=MESH,
        )

    def y_copy(ref, buf, par, d):
        return pltpu.make_async_remote_copy(
            ref.at[pl.ds(buf + H, PL), pl.ds((H if d == 0 else ROWS) * F, H * F)],
            ref.at[pl.ds(buf + H, PL), pl.ds((ER - H if d == 0 else 0) * F, H * F)],
            y_s.at[d],
            y_r.at[par, d],
            device_id=(tms[d], gx),
            device_id_type=MESH,
        )

    def c_copy(ref, buf, par, d, e):
        n = H - 1
        return pltpu.make_async_remote_copy(
            ref.at[pl.ds(buf + (H if d == 0 else PL + 1), n), pl.ds((H if e == 0 else ROWS + 1) * F, n * F)],
            ref.at[pl.ds(buf + (EP - H if d == 0 else 1), n), pl.ds((ER - H if e == 0 else 1) * F, n * F)],
            c_s.at[d, e],
            c_r.at[par, d, e],
            device_id=(tms[e], gxs[d]),
            device_id_type=MESH,
        )

    def x_start(ref, buf, par, i):
        for e in range(2):
            for d in range(2):
                pl.when(x_to[d])(lambda d=d, e=e: x_copy(ref, buf, par, d, e, i).start())

    def x_wait_send(ref, buf, par, i):
        for e in range(2):
            for d in range(2):
                pl.when(x_to[d])(lambda d=d, e=e: x_copy(ref, buf, par, d, e, i).wait_send())

    def x_wait_recv(ref, buf, par, i):
        for e in range(2):
            for d in range(2):
                pl.when(x_from[d])(lambda d=d, e=e: x_copy(ref, buf, par, d, e, i).wait_recv())

    def y_relay(ref, buf, turn, d):
        return pltpu.make_async_remote_copy(
            ref.at[pl.ds(buf + H, PL), pl.ds((H if d == 0 else ROWS) * F, H * F)],
            passing.at[turn],
            y_s.at[d],
            p_r.at[turn],
            device_id=(10 - tm, side),
            device_id_type=MESH,
        )

    def y_forward(ref, buf, turn, par, d):
        return pltpu.make_async_remote_copy(
            passing.at[turn],
            ref.at[pl.ds(buf + H, PL), pl.ds((ER - H if d == 0 else 0) * F, H * F)],
            p_s.at[0],
            y_r.at[par, d],
            device_id=(tm, side),
            device_id_type=MESH,
        )

    def c_forward(ref, buf, turn, par, d, e):
        n = H - 1
        return pltpu.make_async_remote_copy(
            passing.at[turn, pl.ds(0 if d == 0 else PL - n, n), pl.ds((0 if e == 0 else 1) * F, n * F)],
            ref.at[pl.ds(buf + (EP - H if d == 0 else 1), n), pl.ds((ER - H if e == 0 else 1) * F, n * F)],
            p_s.at[1],
            c_r.at[par, d, e],
            device_id=(tm, side_pair),
            device_id_type=MESH,
        )

    def relay(ref, buf, turn, par, again):
        for e in range(2):

            @pl.when(relaying[e])
            def _():
                y_relay(ref, buf, turn, e).wait_recv()
                if again:
                    y_forward(ref, buf, turn, par, e).wait_send()
                    c_forward(ref, buf, turn, par, 0, e).wait_send()
                y_forward(ref, buf, turn, par, e).start()
                pl.when(even)(lambda: c_forward(ref, buf, turn, par, 1, e).start())
                pl.when(~even)(lambda: c_forward(ref, buf, turn, par, 0, e).start())

    def edges_start(ref, buf, turn, par):
        for d in range(2):
            pl.when(y_to[d] & ~relayed[d])(lambda d=d: y_copy(ref, buf, par, d).start())
            pl.when(relayed[d])(lambda d=d: y_relay(ref, buf, turn, d).start())
        for d in range(2):
            for e in range(2):
                pl.when(c_to[d][e])(lambda d=d, e=e: c_copy(ref, buf, par, d, e).start())

    def edges_wait_send(ref, buf, par):
        for d in range(2):
            pl.when(y_to[d])(lambda d=d: y_copy(ref, buf, par, d).wait_send())
        for d in range(2):
            for e in range(2):
                pl.when(c_to[d][e])(lambda d=d, e=e: c_copy(ref, buf, par, d, e).wait_send())

    def edges_wait_recv(ref, buf, par):
        for d in range(2):
            pl.when(y_from[d])(lambda d=d: y_copy(ref, buf, par, d).wait_recv())
        for d in range(2):
            for e in range(2):
                pl.when(x_from[d] & y_from[e])(
                    lambda d=d, e=e: c_copy(ref, buf, par, d, e).wait_recv()
                )

    def parts(ref, base, yi, low, high):
        n = high - low
        at = pl.multiple_of(yi * 8, 8)
        near = ref.at[pl.ds(base + low - 1, n + 2), pl.ds(pl.multiple_of(yi * F - F, 8), 4 * F)]
        vx = fx.at[pl.ds(low, n + 1), pl.ds(at, 16)]
        vy = fy.at[pl.ds(low, n), pl.ds(at, 24)]
        vl = fzl.at[pl.ds(low, n), pl.ds(at, 16)]
        vu = fzu.at[pl.ds(low, n), pl.ds(at, 16)]

        def get(i, r, t):
            return near[i, pl.ds(r * F + 8 * t, 8), :]

        def row(i):
            return [[get(i, r, t) for t in range(2)] for r in (1, 2)]

        below, here = row(0), row(1)
        face_low = [vx[0, pl.ds(8 * r, 8), :] for r in range(2)]
        for i in range(n):
            above = row(i + 2)
            face_high = [vx[i + 1, pl.ds(8 * r, 8), :] for r in range(2)]
            face_y = [vy[i, pl.ds(8 * r, 8), :] for r in range(3)]
            sums = []
            for r in range(2):
                z_low = vl[i, pl.ds(8 * r, 8), :]
                z_high = vu[i, pl.ds(8 * r, 8), :]
                pair = []
                for t in range(2):
                    y_low = get(i + 1, 0, t) if r == 0 else here[0][t]
                    y_high = here[1][t] if r == 0 else get(i + 1, 3, t)
                    pair.append(
                        (face_low[r] * below[r][t] + face_high[r] * above[r][t])
                        + (face_y[r] * y_low + face_y[r + 1] * y_high)
                        + (
                            z_low * pltpu.roll(here[r][t], 1, 1)
                            + z_high * pltpu.roll(here[r][t], 127, 1)
                        )
                    )
                sums.append(pair)
            yield i, here, sums
            below, here, face_low = here, above, face_high

    def inverses(yi, low, high):
        views = [
            c.at[pl.ds(low, high - low), pl.ds(pl.multiple_of(yi * 8, 8), 16)] for c in (ia, ib, ic)
        ]

        def divided(i, r, value):
            a, b, c = [v[i, pl.ds(8 * r, 8), :] for v in views]
            return a * value[0] - b * value[1], c * value[1] + b * value[0]

        return divided

    def starts(yi):
        low, high = H, EP - H
        divided = inverses(yi, low, high)
        vd = dg.at[pl.ds(low, PL), pl.ds(pl.multiple_of(yi * 8, 8), 16)]
        v0 = w0.at[pl.ds(low, PL), pl.ds(pl.multiple_of(yi * F, 8), 2 * F)]
        for i, here, sums in parts(sb, 0, yi, low, high):
            for r in range(2):
                diag = vd[i, pl.ds(8 * r, 8), :]
                spots = [pl.ds(r * F + 8 * t, 8) for t in range(2)]
                right = [
                    v0[i, spots[t], :] - (diag * here[r][t] - sums[r][t]) for t in range(2)
                ]
                value = divided(i, r, right)
                for t in range(2):
                    v0[i, spots[t], :] = value[t]

    def sweep(ref, base, target, target_base, yi, low, high, omega):
        divided = inverses(yi, low, high)
        n = high - low
        rows = pl.ds(pl.multiple_of(yi * F, 8), 2 * F)
        v0 = w0.at[pl.ds(low, n), rows]
        new = target.at[pl.ds(target_base + low, n), rows]
        for i, here, sums in parts(ref, base, yi, low, high):
            for r in range(2):
                step = divided(i, r, sums[r])
                for t in range(2):
                    spot = pl.ds(r * F + 8 * t, 8)
                    new[i, spot, :] = (1.0 - omega) * here[r][t] + omega * (
                        v0[i, spot, :] + step[t]
                    )

    def over(begin, count, body):
        def each(r, _):
            body(begin + 2 * r + H)
            return 0

        lax.fori_loop(0, count // 2, each, 0)

    def start_phase(i):
        over(R * i, R, starts)
        over(ROWS - R - R * i, R, starts)
        if isinstance(i, int):
            edges_start(w0, 0, 0, 0)
        x_start(w0, 0, 0, i)

    for copy in own:
        copy.wait()
    for j in range(7):
        weight_out(j).wait_recv()
    for tiles in (TILE_ORDER[:2], TILE_ORDER[2:]):
        for tile in tiles:
            for j in range(7):
                tile_out(j, tile).wait_recv()
            forward(tile)
            for d in range(2):
                pl.when(x_to[d])(lambda d=d, tile=tile: h_copy(d, tile).start())
            if tile == 0:
                hy_start(0)
            if tile == 3:
                hy_start(1)
    for e in range(2):

        @pl.when(relaying[e])
        def _():
            hy_relay(e).wait_recv()
            hy_forward(e).start()

    for tiles in (TILE_ORDER[:2], TILE_ORDER[2:]):
        for tile in tiles:
            for d in range(2):
                pl.when(x_from[d])(lambda d=d, tile=tile: h_copy(d, tile).wait_recv())
            if tile == 0:
                pl.when(y_from[1])(lambda: hy_copy(1).wait_recv())
            if tile == 3:
                pl.when(y_from[0])(lambda: hy_copy(0).wait_recv())
        if tiles[0] == 0:
            start_phase(0)
            lax.fori_loop(1, NPH // 2, lambda i, _: (start_phase(i), 0)[1], 0)
        else:
            lax.fori_loop(NPH // 2, NPH, lambda i, _: (start_phase(i), 0)[1], 0)
    relay(w0, 0, 0, 0, False)
    for tile in range(4):
        for d in range(2):
            pl.when(x_to[d])(lambda d=d, tile=tile: h_copy(d, tile).wait_send())
    for d in range(2):
        pl.when(y_to[d])(lambda d=d: hy_copy(d).wait_send())

    def home(tile, j):
        return pltpu.make_async_remote_copy(
            stage.at[pl.ds(2 * peers[j], 2), :, pl.ds(pl.multiple_of(8 * tile, 8), 8)],
            out.at[:, :, pl.ds(pl.multiple_of(row0 + 8 * tile, 8), 8)],
            o_s.at[j, tile],
            o_r.at[j, tile],
            device_id=(peers[j], gx),
            device_id_type=MESH,
        )

    def home_recv(tile, j):
        return pltpu.make_async_remote_copy(
            stage.at[pl.ds(2 * tm, 2), :, pl.ds(pl.multiple_of(8 * tile, 8), 8)],
            out.at[:, :, pl.ds(pl.multiple_of(snake(peers[j]) * ROWS + 8 * tile, 8), 8)],
            o_s.at[j, tile],
            o_r.at[j, tile],
            device_id=(peers[j], gx),
            device_id_type=MESH,
        )

    def home_own(tile):
        return pltpu.make_async_copy(
            stage.at[pl.ds(2 * tm, 2), :, pl.ds(pl.multiple_of(8 * tile, 8), 8)],
            out.at[:, :, pl.ds(pl.multiple_of(row0 + 8 * tile, 8), 8)],
            o_l.at[tile],
        )

    def backward(buf, tile):
        rows = pl.multiple_of(tile * 8, 8)

        def plane(x, _):
            base = (8 * tile + H) * F
            field = [w[buf + x + H, pl.ds(base + f, 8, stride=F), :] for f in range(F)]
            modes = [(field[0], None)]
            modes += [(field[m], field[8 + m]) for m in range(1, 8)]
            modes += [(field[8], None)]
            back = real_sum(modes, 16)
            for t in range(16):
                stage[t, x, pl.ds(rows, 8), :] = stage[t, x, pl.ds(rows, 8), :] + back[t] / (
                    16.0 * tws[t]
                )
            return 0

        lax.fori_loop(0, PL, plane, 0)
        for j in range(7):
            home(tile, j).start()
        home_own(tile).start()

    def step(k, _):
        par = lax.rem(k, 2)
        source = par * EP
        result = (1 - par) * EP
        omegas = [pick(OMEGAS[turn::H], k) for turn in range(H)]

        def sweeps(begins, counts):
            for turn in range(H):
                low, high = turn + 1, EP - turn - 1
                for begin in begins[turn]:

                    def run(ref, base, begin=begin, turn=turn, low=low, high=high):
                        last = turn == H - 1
                        target, target_base = (w, result) if last else (wb, turn * EP)
                        over(
                            begin,
                            counts[turn],
                            lambda yi: sweep(
                                ref, base, target, target_base, yi, low, high, omegas[turn]
                            ),
                        )

                    if turn == 0:
                        pl.when(k == 0)(lambda: run(w0, 0))
                        pl.when(k > 0)(lambda: run(w, source))
                    else:
                        run(wb, (turn - 1) * EP)

        def pass_on(i):
            x_wait_send(w, result, par, i)

            @pl.when(k < STEPS - 1)
            def _():
                x_start(w, result, 1 - par, i)

        def finish(i):
            @pl.when(k == STEPS - 1)
            def _():
                backward(result, i)
                backward(result, 3 - i)

        rest = [H - 1 - turn for turn in range(H)]
        edges_wait_recv(w, source, par)
        x_wait_recv(w, source, par, 0)
        x_wait_recv(w, source, par, 1)
        sweeps([(-g, ROWS - R - g) for g in rest], [R + 2 * g for g in rest])
        edges_wait_send(w, result, par)

        @pl.when(k < STEPS - 1)
        def _():
            edges_start(w, result, k + 1, 1 - par)

        pass_on(0)

        def phase(i, _):
            x_wait_recv(w, source, par, i + 1)
            sweeps([(R * i + g, ROWS - R - R * i - g) for g in rest], [R] * H)
            @pl.when((i == NPH - 2) & (k < STEPS - 1))
            def _():
                relay(w, result, k + 1, 1 - par, True)

            pass_on(i)

            @pl.when(i == NPH // 2 - 1)
            def _():
                finish(0)

            return 0

        lax.fori_loop(1, NPH - 1, phase, 0)
        sweeps([(16 - R + g,) for g in rest], [2 * R - 2 * g for g in rest])
        pass_on(NPH - 1)
        finish(1)
        return 0

    lax.fori_loop(0, STEPS, step, 0)

    for e in range(2):

        @pl.when(relaying[e])
        def _():
            hy_forward(e).wait_send()
            y_forward(w, 0, 0, 0, e).wait_send()
            c_forward(w, 0, 0, 0, 0, e).wait_send()

    for j in range(7):
        weight_out(j).wait_send()
        for tile in range(4):
            tile_out(j, tile).wait_send()
    for tile in TILE_ORDER:
        home_own(tile).wait()
        for j in range(7):
            home(tile, j).wait_send()
            home_recv(tile, j).wait_recv()


def shards(ngx, state, start_field, diffusivity, time_weights, shift_real, shift_imag):
    dma = pltpu.SemaphoreType.DMA
    hbm = pl.BlockSpec(memory_space=pltpu.HBM)
    coefficient = pltpu.VMEM((EP, ER * 8, 128), F32)
    return pl.pallas_call(
        functools.partial(kernel, ngx),
        out_shape=jax.ShapeDtypeStruct(state.shape, F32),
        in_specs=[hbm] * 6,
        out_specs=hbm,
        scratch_shapes=[
            pltpu.SMEM((2,), F32),
            pltpu.SMEM((16,), F32),
            pltpu.SMEM((16,), F32),
            pltpu.VMEM((2 * EP, ER * F, 128), F32),
            pltpu.VMEM((EP, ER * F, 128), F32),
            pltpu.VMEM(((H - 1) * EP, ER * F, 128), F32),
            pltpu.VMEM((EP, ER * F, 128), F32),
            pltpu.VMEM((16, PL, ROWS, 128), F32),
            pltpu.VMEM((PL, ROWS, 128), F32),
            pltpu.VMEM((EP, ROWS + 16, 128), F32),
            pltpu.VMEM((16, 8, 128), F32),
            pltpu.VMEM((3, 8, 128), F32),
        ]
        + [coefficient] * 8
        + [
            dma((8,)),
            dma((7, 4)),
            dma((7, 4)),
            dma((7,)),
            dma((7,)),
            dma((2, 3)),
            dma((2, 3)),
            dma((2, 4)),
            dma((2, 4)),
            dma((2,)),
            dma((2,)),
            dma((2, 2, NPH)),
            dma((2, 2, 2, NPH)),
            dma((2,)),
            dma((2, 2)),
            dma((2, 2)),
            dma((2, 2, 2)),
            dma((7, 4)),
            dma((7, 4)),
            dma((4,)),
            pltpu.VMEM((STEPS, PL, H * F, 128), F32),
            pltpu.VMEM((PL, F, 128), F32),
            dma((3,)),
            dma((STEPS + 1,)),
        ],
        compiler_params=pltpu.CompilerParams(
            collective_id=0, has_side_effects=True, vmem_limit_bytes=56 * 2**20
        ),
        cost_estimate=pl.CostEstimate(
            flops=200_000_000, bytes_accessed=4 * 2**20, transcendentals=0
        ),
    )(state, start_field, diffusivity, time_weights, shift_real, shift_imag)


def solution(mesh):
    in_specs = (
        P("tm", "gx", None, None),
        P("gx", None, None),
        P("gx", None, None),
        P("tm"),
        P(),
        P(),
    )
    return jax.shard_map(
        functools.partial(shards, mesh.shape["gx"]),
        mesh=mesh,
        in_specs=in_specs,
        out_specs=P("tm", "gx", None, None),
        check_vma=False,
    )
```

```python
import functools
import math

import jax
import jax.numpy as jnp
from jax import lax
from jax.experimental import pallas as pl
from jax.experimental.pallas import tpu as pltpu
from jax.sharding import PartitionSpec as P

SWEEPS = 12
MESH = pl.DeviceIdType.MESH
F32 = jnp.float32
OMEGAS = [
    1.0 / (1.0 + 0.7 * math.cos(math.pi * (2 * turn + 1) / (2 * SWEEPS))) for turn in range(SWEEPS)
]

TMS = 8
PL = 4
ROWS = 32
H = 4
EP = PL + 2 * H
ER = ROWS + 2 * H
F = 16
R = 4
NPH = 16 // R
STEPS = SWEEPS // H
TILE_ORDER = (0, 3, 1, 2)
PEERS = ((0, 1), (0, 3), (1, 0), (1, 1), (1, 3), (0, 2), (1, 2))


def real_dft(values):
    n = len(values)
    if n == 2:
        return [(values[0] + values[1], None), (values[0] - values[1], None)]
    even = real_dft(values[0::2])
    odd = real_dft(values[1::2])
    half = n // 2
    out = [None] * (half + 1)
    for k in range(half // 2 + 1):
        er, ei = even[k]
        orr, oi = odd[k]
        if k == 0:
            out[0] = (er + orr, None)
            out[half] = (er - orr, None)
        elif 2 * k == half:
            out[k] = (er, -orr)
        else:
            c, s = math.cos(2 * math.pi * k / n), -math.sin(2 * math.pi * k / n)
            if oi is None:
                tr, ti = orr * c, orr * s
            else:
                tr, ti = orr * c - oi * s, orr * s + oi * c
            out[k] = (er + tr, ti if ei is None else ei + ti)
            out[half - k] = (er - tr, ti if ei is None else ti - ei)
    return out


def real_sum(modes, n):
    if n == 2:
        return [modes[0][0] + modes[1][0], modes[0][0] - modes[1][0]]
    half = n // 2
    even, odd = [], []
    for k in range(half // 2 + 1):
        ar, ai = modes[k]
        br, bi = modes[half - k]
        if k == 0:
            even.append((ar + br, None))
            odd.append((ar - br, None))
        elif 2 * k == half:
            even.append((ar + ar, None))
            odd.append((-(ai + ai), None))
        else:
            c, s = math.cos(2 * math.pi * k / n), math.sin(2 * math.pi * k / n)
            even.append((ar + br, ai - bi))
            dr, di = ar - br, ai + bi
            odd.append((dr * c - di * s, dr * s + di * c))
    e = real_sum(even, half)
    o = real_sum(odd, half)
    out = [None] * n
    out[0::2] = e
    out[1::2] = o
    return out


def snake(p):
    return jnp.where(p < 4, p, 11 - p)


def pick(table, index):
    value = jnp.float32(table[0])
    for i in range(1, len(table)):
        value = jnp.where(index == i, jnp.float32(table[i]), value)
    return value


def kernel(
    ngx,
    state,
    start,
    kappa,
    weights_in,
    shift_real_in,
    shift_imag_in,
    out,
    weights,
    shift_real,
    shift_imag,
    w,
    w0,
    wb,
    sb,
    stage,
    first,
    kst,
    tws,
    shifts,
    fx,
    fy,
    fzl,
    fzu,
    dg,
    ia,
    ib,
    ic,
    loc,
    a_s,
    a_r,
    t_s,
    t_r,
    k_s,
    k_r,
    h_s,
    h_r,
    hy_s,
    hy_r,
    x_s,
    x_r,
    y_s,
    y_r,
    c_s,
    c_r,
    o_s,
    o_r,
    o_l,
    passing,
    passing_row,
    p_s,
    p_r,
):
    tm = lax.axis_index("tm")
    gx = lax.axis_index("gx")
    p = snake(tm)
    zh = tm // 4
    xx = lax.rem(tm, 4)
    peers = [lax.rem(zh + dz, 2) * 4 + lax.rem(xx + dx, 4) for dz, dx in PEERS]
    has_lo, has_hi = gx > 0, gx < ngx - 1
    has_dn, has_up = p > 0, p < TMS - 1
    gxs = (gx - 1, gx + 1)
    tms = (snake(p - 1), snake(p + 1))
    x_to = (has_lo, has_hi)
    x_from = (has_hi, has_lo)
    y_to = (has_dn, has_up)
    y_from = (has_up, has_dn)
    row0 = pl.multiple_of(p * ROWS, ROWS)

    turning = (tm == 3) | (tm == 7)
    side = jnp.where(gx < ngx // 2, gx + ngx // 2, gx - ngx // 2)
    side_pair = side + 1 - 2 * lax.rem(side, 2)
    at_end = (gx < 2) | (gx >= ngx - 2)
    relayed = tuple(at_end & (tm == turn) for turn in (7, 3))
    relaying = tuple((gx >= ngx // 2 - 2) & (gx < ngx // 2 + 2) & (tm == turn) for turn in (3, 7))
    even = lax.rem(gx, 2) == 0
    c_to = [
        [
            x_to[d] & y_to[e] & jnp.logical_not(relayed[e] & (even if d == 1 else ~even))
            for e in range(2)
        ]
        for d in range(2)
    ]

    barrier = pltpu.get_barrier_semaphore()
    for peer in peers:
        pl.semaphore_signal(barrier, inc=1, device_id=(peer, gx), device_id_type=MESH)
    for d in range(2):

        @pl.when(x_to[d])
        def _():
            pl.semaphore_signal(barrier, inc=1, device_id=(tm, gxs[d]), device_id_type=MESH)

        for e in range(2):

            @pl.when(x_to[d] & y_to[e])
            def _():
                pl.semaphore_signal(
                    barrier, inc=1, device_id=(tms[e], gxs[d]), device_id_type=MESH
                )

    in_relay = turning & (at_end | ((gx >= ngx // 2 - 2) & (gx < ngx // 2 + 2)))

    @pl.when(in_relay)
    def _():
        for there in ((10 - tm, side), (tm, side), (tm, side_pair)):
            pl.semaphore_signal(barrier, inc=1, device_id=there, device_id_type=MESH)

    nx = has_lo.astype(jnp.int32) + has_hi.astype(jnp.int32)
    ny = has_dn.astype(jnp.int32) + has_up.astype(jnp.int32)

    own = [
        pltpu.make_async_copy(
            state.at[:, :, pl.ds(row0, ROWS)], stage.at[pl.ds(2 * tm, 2)], loc.at[0]
        ),
        pltpu.make_async_copy(start.at[:, pl.ds(row0, ROWS)], first, loc.at[1]),
    ]
    scalars = [
        pltpu.make_async_copy(source, target, loc.at[5 + i])
        for i, (source, target) in enumerate(
            ((weights_in, weights), (shift_real_in, shift_real), (shift_imag_in, shift_imag))
        )
    ]
    for copy in scalars + own:
        copy.start()
    pieces = (
        (None, row0, 8, ROWS),
        (has_dn, pl.multiple_of(jnp.maximum(row0 - 8, 0), 8), 0, 8),
        (has_up, pl.multiple_of(jnp.minimum(row0 + ROWS, (TMS - 1) * ROWS), 8), 8 + ROWS, 8),
    )

    def guarded(condition, body):
        if condition is None:
            body()
        else:
            pl.when(condition)(body)

    def kappa_own(i):
        _, r, at, n = pieces[i]
        return pltpu.make_async_copy(
            kappa.at[:, pl.ds(r, n)], kst.at[pl.ds(H, PL), pl.ds(at, n)], loc.at[2 + i]
        )

    def kappa_out(d, i):
        _, r, at, n = pieces[i]
        return pltpu.make_async_remote_copy(
            kappa.at[pl.ds(0 if d == 0 else PL - H, H), pl.ds(r, n)],
            kst.at[pl.ds(EP - H if d == 0 else 0, H), pl.ds(at, n)],
            k_s.at[d, i],
            k_r.at[d, i],
            device_id=(tm, gxs[d]),
            device_id_type=MESH,
        )

    for i in range(3):
        guarded(pieces[i][0], lambda i=i: kappa_own(i).start())

    pl.semaphore_wait(barrier, 7 + nx + nx * ny + 3 * in_relay.astype(jnp.int32))

    def tile_out(j, tile):
        rows = pl.multiple_of(snake(peers[j]) * ROWS + 8 * tile, 8)
        return pltpu.make_async_remote_copy(
            state.at[:, :, pl.ds(rows, 8)],
            stage.at[pl.ds(2 * tm, 2), :, pl.ds(8 * tile, 8)],
            a_s.at[j, tile],
            a_r.at[j, tile],
            device_id=(peers[j], gx),
            device_id_type=MESH,
        )

    def weight_out(j):
        return pltpu.make_async_remote_copy(
            tws.at[pl.ds(2 * tm, 2)],
            tws.at[pl.ds(2 * tm, 2)],
            t_s.at[j],
            t_r.at[j],
            device_id=(peers[j], gx),
            device_id_type=MESH,
        )

    for d in range(2):
        for i in range(3):
            condition = x_to[d] if pieces[i][0] is None else x_to[d] & pieces[i][0]
            guarded(condition, lambda d=d, i=i: kappa_out(d, i).start())
    for tile in TILE_ORDER:
        for j in range(7):
            tile_out(j, tile).start()
        if tile == 0:
            for copy in scalars:
                copy.wait()
            for i in range(2):
                tws[2 * tm + i] = jnp.full((8, 128), weights[i], F32)
            for j in range(7):
                weight_out(j).start()

    def clear_planes(ref, base, at):
        def body(r, _):
            for i in range(H):
                ref[base + at + i, pl.ds(pl.multiple_of(r * 32, 32), 32)] = jnp.zeros((32, 128), F32)
            return 0

        lax.fori_loop(0, ER * F // 32, body, 0)

    def clear_rows(ref, base, at):
        def body(i, _):
            ref[base + i, pl.ds(at * F, H * F)] = jnp.zeros((H * F, 128), F32)
            return 0

        lax.fori_loop(0, EP, body, 0)

    def clear(condition, planes, at):
        @pl.when(condition)
        def _():
            for i in range(2):
                (clear_planes if planes else clear_rows)(w, i * EP, at)
            (clear_planes if planes else clear_rows)(w0, 0, at)
            (clear_planes if planes else clear_rows)(sb, 0, at)

    clear(gx == 0, True, 0)
    clear(gx == ngx - 1, True, EP - H)
    clear(p == 0, False, 0)
    clear(p == TMS - 1, False, ER - H)
    for condition, at in ((gx == 0, 0), (gx == ngx - 1, EP - H)):

        @pl.when(condition)
        def _():
            kst[pl.ds(at, H)] = jnp.zeros((H, ROWS + 16, 128), F32)

    for condition, at in ((p == 0, 0), (p == TMS - 1, 8 + ROWS)):

        @pl.when(condition)
        def _():
            kst[:, pl.ds(at, 8)] = jnp.zeros((EP, 8, 128), F32)

    lane = lax.broadcasted_iota(jnp.int32, (8, 128), 1)
    sub = lax.broadcasted_iota(jnp.int32, (8, 128), 0)
    s_a = jnp.full((8, 128), shift_real[0], F32)
    s_c = jnp.full((8, 128), shift_real[8], F32)
    s_i = jnp.zeros((8, 128), F32)
    for m in range(1, 8):
        s_a = jnp.where(sub == m, shift_real[m], s_a)
        s_c = jnp.where(sub == m, shift_real[m], s_c)
        s_i = jnp.where(sub == m, shift_imag[m], s_i)
    shifts[0] = s_a
    shifts[1] = s_c
    shifts[2] = s_i

    for i in range(3):
        guarded(pieces[i][0], lambda i=i: kappa_own(i).wait())
    for d in range(2):
        for i in range(3):
            cond_from = x_from[d] if pieces[i][0] is None else x_from[d] & pieces[i][0]
            cond_to = x_to[d] if pieces[i][0] is None else x_to[d] & pieces[i][0]
            guarded(cond_from, lambda d=d, i=i: kappa_out(d, i).wait_recv())
            guarded(cond_to, lambda d=d, i=i: kappa_out(d, i).wait_send())

    def coefficients(yi, _):
        at = pl.multiple_of(yi * 8, 8)

        def cell(px, dy):
            return jnp.broadcast_to(kst[px, pl.ds(yi + 8 - H + dy, 1), :], (8, 128))

        s_a, s_c, s_i = shifts[0], shifts[1], shifts[2]
        outside_y = ((p == 0) & (yi < H)) | ((p == TMS - 1) & (yi > ER - 1 - H))
        below, here = cell(0, 0), cell(1, 0)
        low = 0.5 * (here + below)
        for px in range(1, EP - 1):
            above = cell(px + 1, 0)
            high = 0.5 * (here + above)
            yl = 0.5 * (here + cell(px, -1))
            yu = 0.5 * (here + cell(px, 1))
            k_low = jnp.where(lane == 0, 0.0, pltpu.roll(here, 1, 1))
            k_high = jnp.where(lane == 127, 0.0, pltpu.roll(here, 127, 1))
            zl = 0.5 * (here + k_low)
            zu = 0.5 * (here + k_high)
            diag = low + high + yl + yu + zl + zu
            fx[px, pl.ds(at, 8)] = low
            if px == EP - 2:
                fx[px + 1, pl.ds(at, 8)] = high
            fy[px, pl.ds(at, 8)] = yl
            fy[px, pl.ds(pl.multiple_of(at + 8, 8), 8)] = yu
            fzl[px, pl.ds(at, 8)] = jnp.where(lane == 0, 0.0, zl)
            fzu[px, pl.ds(at, 8)] = jnp.where(lane == 127, 0.0, zu)
            dg[px, pl.ds(at, 8)] = diag
            outside = outside_y
            if px < H:
                outside = outside | (gx == 0)
            if px > EP - 1 - H:
                outside = outside | (gx == ngx - 1)
            inside = jnp.where(outside, 0.0, 1.0).astype(F32)
            d_a = s_a + diag
            ratio = inside / (d_a * d_a + s_i * s_i)
            ia[px, pl.ds(at, 8)] = d_a * ratio
            ib[px, pl.ds(at, 8)] = -s_i * ratio
            d_c = s_c + diag
            ic[px, pl.ds(at, 8)] = d_c * (inside / (d_c * d_c + s_i * s_i))
            here, low = above, high
        return 0

    lax.fori_loop(1, ER - 1, coefficients, 0)

    def forward(tile):
        rows = pl.multiple_of(tile * 8, 8)

        def plane(x, _):
            base = (8 * tile + H) * F

            def put(ref, at, modes):
                for m in range(9):
                    re, im = modes[m]
                    if m == 8:
                        ref[at, pl.ds(base + 8, 8, stride=F), :] = re
                        continue
                    ref[at, pl.ds(base + m, 8, stride=F), :] = re
                    if m > 0:
                        ref[at, pl.ds(base + 8 + m, 8, stride=F), :] = im

            now = [stage[t, x, pl.ds(rows, 8), :] for t in range(16)]
            put(sb, x + H, real_dft([tws[t] * now[t] for t in range(16)]))
            before = [first[x, pl.ds(rows, 8), :]] + now[:15]
            put(
                w0,
                x + H,
                real_dft([tws[t] * (before[t] - now[t] * now[t] * now[t]) for t in range(16)]),
            )
            return 0

        lax.fori_loop(0, PL, plane, 0)

    def h_copy(d, tile):
        rows = pl.ds(pl.multiple_of((8 * tile + H) * F, 8), 8 * F)
        return pltpu.make_async_remote_copy(
            sb.at[H if d == 0 else EP - 1 - H, rows],
            sb.at[EP - H if d == 0 else H - 1, rows],
            h_s.at[d, tile],
            h_r.at[d, tile],
            device_id=(tm, gxs[d]),
            device_id_type=MESH,
        )

    def hy_copy(d):
        return pltpu.make_async_remote_copy(
            sb.at[pl.ds(H, PL), pl.ds((H if d == 0 else ER - 1 - H) * F, F)],
            sb.at[pl.ds(H, PL), pl.ds((ER - H if d == 0 else H - 1) * F, F)],
            hy_s.at[d],
            hy_r.at[d],
            device_id=(tms[d], gx),
            device_id_type=MESH,
        )

    def hy_relay(d):
        return pltpu.make_async_remote_copy(
            sb.at[pl.ds(H, PL), pl.ds((H if d == 0 else ER - 1 - H) * F, F)],
            passing_row,
            hy_s.at[d],
            p_r.at[STEPS],
            device_id=(10 - tm, side),
            device_id_type=MESH,
        )

    def hy_forward(d):
        return pltpu.make_async_remote_copy(
            passing_row,
            sb.at[pl.ds(H, PL), pl.ds((ER - H if d == 0 else H - 1) * F, F)],
            p_s.at[2],
            hy_r.at[d],
            device_id=(tm, side),
            device_id_type=MESH,
        )

    def hy_start(d):
        pl.when(y_to[d] & ~relayed[d])(lambda: hy_copy(d).start())
        pl.when(relayed[d])(lambda: hy_relay(d).start())

    def x_copy(ref, buf, par, d, e, i):
        r = R * i if e == 0 else ROWS - R - R * i
        rows = pl.ds(pl.multiple_of((r + H) * F, 8), R * F)
        return pltpu.make_async_remote_copy(
            ref.at[pl.ds(buf + (H if d == 0 else PL), H), rows],
            ref.at[pl.ds(buf + (EP - H if d == 0 else 0), H), rows],
            x_s.at[d, e, i],
            x_r.at[par, d, e, i],
            device_id=(tm, gxs[d]),
            device_id_type=MESH,
        )

    def y_copy(ref, buf, par, d):
        return pltpu.make_async_remote_copy(
            ref.at[pl.ds(buf + H, PL), pl.ds((H if d == 0 else ROWS) * F, H * F)],
            ref.at[pl.ds(buf + H, PL), pl.ds((ER - H if d == 0 else 0) * F, H * F)],
            y_s.at[d],
            y_r.at[par, d],
            device_id=(tms[d], gx),
            device_id_type=MESH,
        )

    def c_copy(ref, buf, par, d, e):
        n = H - 1
        return pltpu.make_async_remote_copy(
            ref.at[pl.ds(buf + (H if d == 0 else PL + 1), n), pl.ds((H if e == 0 else ROWS + 1) * F, n * F)],
            ref.at[pl.ds(buf + (EP - H if d == 0 else 1), n), pl.ds((ER - H if e == 0 else 1) * F, n * F)],
            c_s.at[d, e],
            c_r.at[par, d, e],
            device_id=(tms[e], gxs[d]),
            device_id_type=MESH,
        )

    def x_start(ref, buf, par, i):
        for e in range(2):
            for d in range(2):
                pl.when(x_to[d])(lambda d=d, e=e: x_copy(ref, buf, par, d, e, i).start())

    def x_wait_send(ref, buf, par, i):
        for e in range(2):
            for d in range(2):
                pl.when(x_to[d])(lambda d=d, e=e: x_copy(ref, buf, par, d, e, i).wait_send())

    def x_wait_recv(ref, buf, par, i):
        for e in range(2):
            for d in range(2):
                pl.when(x_from[d])(lambda d=d, e=e: x_copy(ref, buf, par, d, e, i).wait_recv())

    def y_relay(ref, buf, turn, d):
        return pltpu.make_async_remote_copy(
            ref.at[pl.ds(buf + H, PL), pl.ds((H if d == 0 else ROWS) * F, H * F)],
            passing.at[turn],
            y_s.at[d],
            p_r.at[turn],
            device_id=(10 - tm, side),
            device_id_type=MESH,
        )

    def y_forward(ref, buf, turn, par, d):
        return pltpu.make_async_remote_copy(
            passing.at[turn],
            ref.at[pl.ds(buf + H, PL), pl.ds((ER - H if d == 0 else 0) * F, H * F)],
            p_s.at[0],
            y_r.at[par, d],
            device_id=(tm, side),
            device_id_type=MESH,
        )

    def c_forward(ref, buf, turn, par, d, e):
        n = H - 1
        return pltpu.make_async_remote_copy(
            passing.at[turn, pl.ds(0 if d == 0 else PL - n, n), pl.ds((0 if e == 0 else 1) * F, n * F)],
            ref.at[pl.ds(buf + (EP - H if d == 0 else 1), n), pl.ds((ER - H if e == 0 else 1) * F, n * F)],
            p_s.at[1],
            c_r.at[par, d, e],
            device_id=(tm, side_pair),
            device_id_type=MESH,
        )

    def relay(ref, buf, turn, par, again):
        for e in range(2):

            @pl.when(relaying[e])
            def _():
                y_relay(ref, buf, turn, e).wait_recv()
                if again:
                    y_forward(ref, buf, turn, par, e).wait_send()
                    c_forward(ref, buf, turn, par, 0, e).wait_send()
                y_forward(ref, buf, turn, par, e).start()
                pl.when(even)(lambda: c_forward(ref, buf, turn, par, 1, e).start())
                pl.when(~even)(lambda: c_forward(ref, buf, turn, par, 0, e).start())

    def edges_start(ref, buf, turn, par):
        for d in range(2):
            pl.when(y_to[d] & ~relayed[d])(lambda d=d: y_copy(ref, buf, par, d).start())
            pl.when(relayed[d])(lambda d=d: y_relay(ref, buf, turn, d).start())
        for d in range(2):
            for e in range(2):
                pl.when(c_to[d][e])(lambda d=d, e=e: c_copy(ref, buf, par, d, e).start())

    def edges_wait_send(ref, buf, par):
        for d in range(2):
            pl.when(y_to[d])(lambda d=d: y_copy(ref, buf, par, d).wait_send())
        for d in range(2):
            for e in range(2):
                pl.when(c_to[d][e])(lambda d=d, e=e: c_copy(ref, buf, par, d, e).wait_send())

    def edges_wait_recv(ref, buf, par):
        for d in range(2):
            pl.when(y_from[d])(lambda d=d: y_copy(ref, buf, par, d).wait_recv())
        for d in range(2):
            for e in range(2):
                pl.when(x_from[d] & y_from[e])(
                    lambda d=d, e=e: c_copy(ref, buf, par, d, e).wait_recv()
                )

    def parts(ref, base, yi, low, high):
        n = high - low
        at = pl.multiple_of(yi * 8, 8)
        near = ref.at[pl.ds(base + low - 1, n + 2), pl.ds(pl.multiple_of(yi * F - F, 8), 4 * F)]
        vx = fx.at[pl.ds(low, n + 1), pl.ds(at, 16)]
        vy = fy.at[pl.ds(low, n), pl.ds(at, 24)]
        vl = fzl.at[pl.ds(low, n), pl.ds(at, 16)]
        vu = fzu.at[pl.ds(low, n), pl.ds(at, 16)]

        def get(i, r, t):
            return near[i, pl.ds(r * F + 8 * t, 8), :]

        def row(i):
            return [[get(i, r, t) for t in range(2)] for r in (1, 2)]

        below, here = row(0), row(1)
        face_low = [vx[0, pl.ds(8 * r, 8), :] for r in range(2)]
        for i in range(n):
            above = row(i + 2)
            face_high = [vx[i + 1, pl.ds(8 * r, 8), :] for r in range(2)]
            face_y = [vy[i, pl.ds(8 * r, 8), :] for r in range(3)]
            sums = []
            for r in range(2):
                z_low = vl[i, pl.ds(8 * r, 8), :]
                z_high = vu[i, pl.ds(8 * r, 8), :]
                pair = []
                for t in range(2):
                    y_low = get(i + 1, 0, t) if r == 0 else here[0][t]
                    y_high = here[1][t] if r == 0 else get(i + 1, 3, t)
                    pair.append(
                        (face_low[r] * below[r][t] + face_high[r] * above[r][t])
                        + (face_y[r] * y_low + face_y[r + 1] * y_high)
                        + (
                            z_low * pltpu.roll(here[r][t], 1, 1)
                            + z_high * pltpu.roll(here[r][t], 127, 1)
                        )
                    )
                sums.append(pair)
            yield i, here, sums
            below, here, face_low = here, above, face_high

    def inverses(yi, low, high):
        views = [
            c.at[pl.ds(low, high - low), pl.ds(pl.multiple_of(yi * 8, 8), 16)] for c in (ia, ib, ic)
        ]

        def divided(i, r, value):
            a, b, c = [v[i, pl.ds(8 * r, 8), :] for v in views]
            return a * value[0] - b * value[1], c * value[1] + b * value[0]

        return divided

    def starts(yi):
        low, high = H, EP - H
        divided = inverses(yi, low, high)
        vd = dg.at[pl.ds(low, PL), pl.ds(pl.multiple_of(yi * 8, 8), 16)]
        v0 = w0.at[pl.ds(low, PL), pl.ds(pl.multiple_of(yi * F, 8), 2 * F)]
        for i, here, sums in parts(sb, 0, yi, low, high):
            for r in range(2):
                diag = vd[i, pl.ds(8 * r, 8), :]
                spots = [pl.ds(r * F + 8 * t, 8) for t in range(2)]
                right = [
                    v0[i, spots[t], :] - (diag * here[r][t] - sums[r][t]) for t in range(2)
                ]
                value = divided(i, r, right)
                for t in range(2):
                    v0[i, spots[t], :] = value[t]

    def sweep(ref, base, target, target_base, yi, low, high, omega):
        divided = inverses(yi, low, high)
        n = high - low
        rows = pl.ds(pl.multiple_of(yi * F, 8), 2 * F)
        v0 = w0.at[pl.ds(low, n), rows]
        new = target.at[pl.ds(target_base + low, n), rows]
        for i, here, sums in parts(ref, base, yi, low, high):
            for r in range(2):
                step = divided(i, r, sums[r])
                for t in range(2):
                    spot = pl.ds(r * F + 8 * t, 8)
                    new[i, spot, :] = (1.0 - omega) * here[r][t] + omega * (
                        v0[i, spot, :] + step[t]
                    )

    def over(begin, count, body):
        def each(r, _):
            body(begin + 2 * r + H)
            return 0

        lax.fori_loop(0, count // 2, each, 0)

    def start_phase(i):
        over(R * i, R, starts)
        over(ROWS - R - R * i, R, starts)
        if isinstance(i, int):
            edges_start(w0, 0, 0, 0)
        x_start(w0, 0, 0, i)

    for copy in own:
        copy.wait()
    for j in range(7):
        weight_out(j).wait_recv()
    for tiles in (TILE_ORDER[:2], TILE_ORDER[2:]):
        for tile in tiles:
            for j in range(7):
                tile_out(j, tile).wait_recv()
            forward(tile)
            for d in range(2):
                pl.when(x_to[d])(lambda d=d, tile=tile: h_copy(d, tile).start())
            if tile == 0:
                hy_start(0)
            if tile == 3:
                hy_start(1)
    for e in range(2):

        @pl.when(relaying[e])
        def _():
            hy_relay(e).wait_recv()
            hy_forward(e).start()

    for tiles in (TILE_ORDER[:2], TILE_ORDER[2:]):
        for tile in tiles:
            for d in range(2):
                pl.when(x_from[d])(lambda d=d, tile=tile: h_copy(d, tile).wait_recv())
            if tile == 0:
                pl.when(y_from[1])(lambda: hy_copy(1).wait_recv())
            if tile == 3:
                pl.when(y_from[0])(lambda: hy_copy(0).wait_recv())
        if tiles[0] == 0:
            start_phase(0)
            lax.fori_loop(1, NPH // 2, lambda i, _: (start_phase(i), 0)[1], 0)
        else:
            lax.fori_loop(NPH // 2, NPH, lambda i, _: (start_phase(i), 0)[1], 0)
    relay(w0, 0, 0, 0, False)
    for tile in range(4):
        for d in range(2):
            pl.when(x_to[d])(lambda d=d, tile=tile: h_copy(d, tile).wait_send())
    for d in range(2):
        pl.when(y_to[d])(lambda d=d: hy_copy(d).wait_send())

    def home(tile, j):
        return pltpu.make_async_remote_copy(
            stage.at[pl.ds(2 * peers[j], 2), :, pl.ds(pl.multiple_of(8 * tile, 8), 8)],
            out.at[:, :, pl.ds(pl.multiple_of(row0 + 8 * tile, 8), 8)],
            o_s.at[j, tile],
            o_r.at[j, tile],
            device_id=(peers[j], gx),
            device_id_type=MESH,
        )

    def home_recv(tile, j):
        return pltpu.make_async_remote_copy(
            stage.at[pl.ds(2 * tm, 2), :, pl.ds(pl.multiple_of(8 * tile, 8), 8)],
            out.at[:, :, pl.ds(pl.multiple_of(snake(peers[j]) * ROWS + 8 * tile, 8), 8)],
            o_s.at[j, tile],
            o_r.at[j, tile],
            device_id=(peers[j], gx),
            device_id_type=MESH,
        )

    def home_own(tile):
        return pltpu.make_async_copy(
            stage.at[pl.ds(2 * tm, 2), :, pl.ds(pl.multiple_of(8 * tile, 8), 8)],
            out.at[:, :, pl.ds(pl.multiple_of(row0 + 8 * tile, 8), 8)],
            o_l.at[tile],
        )

    def backward(buf, tile):
        rows = pl.multiple_of(tile * 8, 8)

        def plane(x, _):
            base = (8 * tile + H) * F
            field = [w[buf + x + H, pl.ds(base + f, 8, stride=F), :] for f in range(F)]
            modes = [(field[0], None)]
            modes += [(field[m], field[8 + m]) for m in range(1, 8)]
            modes += [(field[8], None)]
            back = real_sum(modes, 16)
            for t in range(16):
                stage[t, x, pl.ds(rows, 8), :] = stage[t, x, pl.ds(rows, 8), :] + back[t] / (
                    16.0 * tws[t]
                )
            return 0

        lax.fori_loop(0, PL, plane, 0)
        for j in range(7):
            home(tile, j).start()
        home_own(tile).start()

    def step(k, _):
        par = lax.rem(k, 2)
        source = par * EP
        result = (1 - par) * EP
        omegas = [pick(OMEGAS[turn::H], k) for turn in range(H)]

        def sweeps(begins, counts):
            for turn in range(H):
                low, high = turn + 1, EP - turn - 1
                for begin in begins[turn]:

                    def run(ref, base, begin=begin, turn=turn, low=low, high=high):
                        last = turn == H - 1
                        target, target_base = (w, result) if last else (wb, turn * EP)
                        over(
                            begin,
                            counts[turn],
                            lambda yi: sweep(
                                ref, base, target, target_base, yi, low, high, omegas[turn]
                            ),
                        )

                    if turn == 0:
                        pl.when(k == 0)(lambda: run(w0, 0))
                        pl.when(k > 0)(lambda: run(w, source))
                    else:
                        run(wb, (turn - 1) * EP)

        def pass_on(i):
            x_wait_send(w, result, par, i)

            @pl.when(k < STEPS - 1)
            def _():
                x_start(w, result, 1 - par, i)

        def finish(i):
            @pl.when(k == STEPS - 1)
            def _():
                backward(result, i)
                backward(result, 3 - i)

        rest = [H - 1 - turn for turn in range(H)]
        edges_wait_recv(w, source, par)
        x_wait_recv(w, source, par, 0)
        x_wait_recv(w, source, par, 1)
        sweeps([(-g, ROWS - R - g) for g in rest], [R + 2 * g for g in rest])
        edges_wait_send(w, result, par)

        @pl.when(k < STEPS - 1)
        def _():
            edges_start(w, result, k + 1, 1 - par)

        pass_on(0)

        def phase(i, _):
            x_wait_recv(w, source, par, i + 1)
            sweeps([(R * i + g, ROWS - R - R * i - g) for g in rest], [R] * H)
            @pl.when((i == NPH - 2) & (k < STEPS - 1))
            def _():
                relay(w, result, k + 1, 1 - par, True)

            pass_on(i)

            @pl.when(i == NPH // 2 - 1)
            def _():
                finish(0)

            return 0

        lax.fori_loop(1, NPH - 1, phase, 0)
        sweeps([(16 - R + g,) for g in rest], [2 * R - 2 * g for g in rest])
        pass_on(NPH - 1)
        finish(1)
        return 0

    lax.fori_loop(0, STEPS, step, 0)

    for e in range(2):

        @pl.when(relaying[e])
        def _():
            hy_forward(e).wait_send()
            y_forward(w, 0, 0, 0, e).wait_send()
            c_forward(w, 0, 0, 0, 0, e).wait_send()

    for j in range(7):
        weight_out(j).wait_send()
        for tile in range(4):
            tile_out(j, tile).wait_send()
    for tile in TILE_ORDER:
        home_own(tile).wait()
        for j in range(7):
            home(tile, j).wait_send()
            home_recv(tile, j).wait_recv()


def shards(ngx, state, start_field, diffusivity, time_weights, shift_real, shift_imag):
    dma = pltpu.SemaphoreType.DMA
    hbm = pl.BlockSpec(memory_space=pltpu.HBM)
    coefficient = pltpu.VMEM((EP, ER * 8, 128), F32)
    return pl.pallas_call(
        functools.partial(kernel, ngx),
        out_shape=jax.ShapeDtypeStruct(state.shape, F32),
        in_specs=[hbm] * 6,
        out_specs=hbm,
        scratch_shapes=[
            pltpu.SMEM((2,), F32),
            pltpu.SMEM((16,), F32),
            pltpu.SMEM((16,), F32),
            pltpu.VMEM((2 * EP, ER * F, 128), F32),
            pltpu.VMEM((EP, ER * F, 128), F32),
            pltpu.VMEM(((H - 1) * EP, ER * F, 128), F32),
            pltpu.VMEM((EP, ER * F, 128), F32),
            pltpu.VMEM((16, PL, ROWS, 128), F32),
            pltpu.VMEM((PL, ROWS, 128), F32),
            pltpu.VMEM((EP, ROWS + 16, 128), F32),
            pltpu.VMEM((16, 8, 128), F32),
            pltpu.VMEM((3, 8, 128), F32),
        ]
        + [coefficient] * 8
        + [
            dma((8,)),
            dma((7, 4)),
            dma((7, 4)),
            dma((7,)),
            dma((7,)),
            dma((2, 3)),
            dma((2, 3)),
            dma((2, 4)),
            dma((2, 4)),
            dma((2,)),
            dma((2,)),
            dma((2, 2, NPH)),
            dma((2, 2, 2, NPH)),
            dma((2,)),
            dma((2, 2)),
            dma((2, 2)),
            dma((2, 2, 2)),
            dma((7, 4)),
            dma((7, 4)),
            dma((4,)),
            pltpu.VMEM((STEPS, PL, H * F, 128), F32),
            pltpu.VMEM((PL, F, 128), F32),
            dma((3,)),
            dma((STEPS + 1,)),
        ],
        compiler_params=pltpu.CompilerParams(
            collective_id=0, has_side_effects=True, vmem_limit_bytes=56 * 2**20
        ),
        cost_estimate=pl.CostEstimate(
            flops=200_000_000, bytes_accessed=4 * 2**20, transcendentals=0
        ),
    )(state, start_field, diffusivity, time_weights, shift_real, shift_imag)


def solution(mesh):
    in_specs = (
        P("tm", "gx", None, None),
        P("gx", None, None),
        P("gx", None, None),
        P("tm"),
        P(),
        P(),
    )
    return jax.shard_map(
        functools.partial(shards, mesh.shape["gx"]),
        mesh=mesh,
        in_specs=in_specs,
        out_specs=P("tm", "gx", None, None),
        check_vma=False,
    )
```
